32 devices in a mesh: dp: 16 (over z, y, x), tensor: 2 (over core).
Axes of the slice: x: 2, y: 2, z: 4, core: 2. Of those that a mesh axis runs over, the one named last changes fastest.
Arguments:
- tokens: bfloat16 [10240, 2048], P(('dp', 'tensor')), may hold values from -6 to 6
- seq_ends: int32 [16, 4], P('dp'), may hold values from 128 to 640, as said below
- w_query: bfloat16 [2048, 2048], P('dp', 'tensor'), may hold values from -0.125 to 0.125
- w_key: bfloat16 [2048, 1024], P('dp', 'tensor'), may hold values from -0.125 to 0.125
- w_value: bfloat16 [2048, 1024], P('dp', 'tensor'), may hold values from -0.125 to 0.125
- w_out: bfloat16 [2048, 2048], P('tensor', 'dp'), may hold values from -1 to 1
- w_gate: bfloat16 [2048, 6144], P('dp', 'tensor'), may hold values from -0.125 to 0.125
- w_up: bfloat16 [2048, 6144], P('dp', 'tensor'), may hold values from -0.125 to 0.125
- w_down: bfloat16 [6144, 2048], P('tensor', 'dp'), may hold values from -0.078125 to 0.078125
- gain_attn: float32 [2048], replicated, may hold values from 0.1 to 1.9
- gain_mlp: float32 [2048], replicated, may hold values from 0.1 to 1.9
- gain_query: float32 [128], replicated, may hold values from 0.1 to 1.9
- gain_key: float32 [128], replicated, may hold values from 0.1 to 1.9
- cotangent: bfloat16 [10240, 2048], P(('dp', 'tensor')), may hold values from -6 to 6
Outputs:
- out_tokens: bfloat16 [10240, 2048], P(('dp', 'tensor'))
- grad_tokens: float32 [10240, 2048], P(('dp', 'tensor'))
- grad_query: float32 [2048, 2048], P('dp', 'tensor')
- grad_key: float32 [2048, 1024], P('dp', 'tensor')
- grad_value: float32 [2048, 1024], P('dp', 'tensor')
- grad_out: float32 [2048, 2048], P('tensor', 'dp')
- grad_gate: float32 [2048, 6144], P('dp', 'tensor')
- grad_up: float32 [2048, 6144], P('dp', 'tensor')
- grad_down: float32 [6144, 2048], P('tensor', 'dp')
- grad_gain_attn: float32 [2048], replicated
- grad_gain_mlp: float32 [2048], replicated
- grad_gain_query: float32 [128], replicated
- grad_gain_key: float32 [128], replicated
The draws below stay inside these ranges and needn't reach their ends.
Inputs may be any that keep to these rules, and one draw needn't show every extreme that they name: `seq_ends`: each row rises strictly and every entry is a multiple of 128, so every sequence is a whole number of 128-slot blocks, one block or more. The last entry is the group's used slots: at least 512, more than 320, and equal to 640 in some group. No entry other than the last equals 320, so one sequence of every group spans slots 320 - 1 and 320.
All inputs are finite; a program needn't handle non-finite values.
Results may differ from the reference program's by a relative error of at most 0.015.
Values may be sent and summed in bfloat16 or wider, within the bound.
No kernel may reach another device: no remote copies, remote signals or barrier semaphores. Data moves between devices by JAX's collectives and lax.ppermute only.
A program may use at most 256 MiB of HBM per device.

```python
import jax
import jax.numpy as jnp
from jax import lax

D = 2048
HEADS = 16
KV = 8
HD = 128
FF = 6144
CAP = 640
NSEQ = 4
BLOCK = 128
HALF = 320
TOKENS = 10240
N_DP = 16


def draw_seq_ends(key, part):
    key = jax.random.fold_in(key, 11)
    used_key, full_key, cut_key = jax.random.split(key, 3)
    block_count = CAP // BLOCK
    lowest_blocks = max(NSEQ, (CAP - HALF) // BLOCK + 1)
    if HALF % BLOCK == 0:
        lowest_blocks = max(lowest_blocks, NSEQ + 1)
    used = jax.random.randint(used_key, (N_DP,), lowest_blocks, block_count + 1) * BLOCK
    full_group = jax.random.randint(full_key, (), 0, N_DP)
    used = jnp.where(jnp.arange(N_DP) == full_group, CAP, used)

    def one_group(sub_key, used_top):
        order = jax.random.permutation(sub_key, block_count - 1) + 1
        bounds = order * BLOCK
        valid = (bounds < used_top) & (bounds != HALF)
        ranks = jnp.arange(block_count - 1)
        score = jnp.where(valid, ranks, ranks + block_count)
        picked = jnp.argsort(score)[:NSEQ - 1]
        cuts = jnp.sort(bounds[picked])
        return jnp.concatenate([cuts, used_top[None]]).astype(jnp.int32)
    return jax.vmap(one_group)(jax.random.split(cut_key, N_DP), used)


def level_of(key, dims, cuts, least, high):
    level, own = 1.0, jax.random.fold_in(key, 6)
    for position, blocks in cuts:
        heights = jnp.exp(jax.random.uniform(jax.random.fold_in(own, position), (blocks,), jnp.float32, least / len(cuts), high / len(cuts)))
        level = level * jnp.repeat(heights, dims[position] // blocks).reshape([-1 if axis == position else 1 for axis in range(len(dims))])
    return level


def scatter_about(stream_key, extent, scale, bound, shards=(), kind=jnp.bfloat16):
    entries = scale * jax.random.normal(stream_key, extent, jnp.float32)
    if shards:
        entries = entries * level_of(stream_key, extent, shards, -0.22, 0.18)
    return jnp.clip(entries, -bound, bound).astype(kind)


def setup_inputs(seed: int = 0) -> dict:
    seeds = jax.random.split(jax.random.key(seed), 15)
    return {
        "tokens": scatter_about(seeds[0], (TOKENS, D), 1.0, 6.0, ((0, 32),)),
        "seq_ends": draw_seq_ends(jax.random.fold_in(seeds[14], 71), 0),
        "w_query": scatter_about(seeds[2], (D, HEADS * HD), D ** -0.5, 0.125, ((0, 16), (1, 2))),
        "w_key": scatter_about(seeds[3], (D, KV * HD), D ** -0.5, 0.125, ((0, 16), (1, 2))),
        "w_value": scatter_about(seeds[4], (D, KV * HD), D ** -0.5, 0.125, ((0, 16), (1, 2))),
        "w_out": scatter_about(seeds[5], (HEADS * HD, D), (max(HEADS * HD // 64, 4)) ** -0.5, 1.0, ((0, 2), (1, 16))),
        "w_gate": scatter_about(seeds[6], (D, FF), D ** -0.5, 0.125, ((0, 16), (1, 2))),
        "w_up": scatter_about(seeds[7], (D, FF), D ** -0.5, 0.125, ((0, 16), (1, 2))),
        "w_down": scatter_about(seeds[8], (FF, D), FF ** -0.5, 0.078125, ((0, 2), (1, 16))),
        "gain_attn": jnp.clip(1.0 + 0.18 * jax.random.normal(seeds[9], (D,), jnp.float32), 0.1, 1.9),
        "gain_mlp": jnp.clip(1.0 + 0.18 * jax.random.normal(seeds[10], (D,), jnp.float32), 0.1, 1.9),
        "gain_query": jnp.clip(1.0 + 0.18 * jax.random.normal(seeds[11], (HD,), jnp.float32), 0.1, 1.9),
        "gain_key": jnp.clip(1.0 + 0.18 * jax.random.normal(seeds[12], (HD,), jnp.float32), 0.1, 1.9),
        "cotangent": scatter_about(seeds[13], (TOKENS, D), 1.0, 6.0, ((0, 32),)),
    }


EPSILON = 1e-06
ROPE_BASE = 1000000.0
HIGHEST = lax.Precision.HIGHEST

@jax.custom_vjp
def low(v):
    return lax.optimization_barrier(v.astype(jnp.bfloat16)).astype(jnp.float32)

@jax.custom_vjp
def low_back(v):
    return v

def low_keep(v):
    return (low(v), None)

def low_pass(kept, grad):
    return (grad,)

def back_keep(v):
    return (v, None)

def back_low(kept, grad):
    return (low(grad),)
low.defvjp(low_keep, low_pass)
low_back.defvjp(back_keep, back_low)

def matmul(left, right):
    return jnp.dot(left, right, precision=HIGHEST)

def rms_norm(values, gain_vec):
    return values * lax.rsqrt(lax.optimization_barrier(jnp.mean(values * values, axis=-1, keepdims=True)) + EPSILON) * gain_vec

def rotary(values, cosine_table, sine_table):
    half_width = values.shape[-1] // 2
    front_half = values[..., :half_width]
    back_half = values[..., half_width:]
    cosine_table = cosine_table[:, None, :]
    sine_table = sine_table[:, None, :]
    return jnp.concatenate([front_half * cosine_table - back_half * sine_table, back_half * cosine_table + front_half * sine_table], axis=-1)

def rope_tables(positions, width):
    half_width = width // 2
    frequency = ROPE_BASE ** (-2.0 * jnp.arange(half_width, dtype=jnp.float32) / width)
    angles = positions.astype(jnp.float32)[:, None] * frequency[None, :]
    return (jnp.cos(angles), jnp.sin(angles))

def token_layout(seq_ends, slot_count):
    token_index = jnp.arange(slot_count, dtype=jnp.int32)
    segment = lax.optimization_barrier(jnp.sum((token_index[:, None] >= seq_ends[None, :]).astype(jnp.int32), axis=1))
    starts = jnp.concatenate([jnp.zeros((1,), jnp.int32), seq_ends[:-1].astype(jnp.int32)])
    onehot = (segment[:, None] == jnp.arange(seq_ends.shape[0], dtype=jnp.int32)[None, :]).astype(jnp.int32)
    positions = token_index - lax.optimization_barrier(jnp.sum(onehot * starts[None, :], axis=1))
    return (segment, positions)

def attend(query_heads, key_heads, value_heads, segment, live_rows):
    rows_count = query_heads.shape[0]
    grouped = query_heads.reshape(rows_count, key_heads.shape[1], -1, key_heads.shape[2])
    scores = low_back(jnp.einsum('qkgd,skd->kgqs', grouped, key_heads, precision=HIGHEST) * key_heads.shape[2] ** (-0.5))
    places = jnp.arange(rows_count, dtype=jnp.int32)
    allowed = (segment[:, None] == segment[None, :]) & (places[None, :] <= places[:, None]) & live_rows[:, None]
    masked = jnp.where(allowed, scores, -1e+30)
    row_max = lax.optimization_barrier(jnp.max(masked, axis=-1, keepdims=True))
    weights = jnp.exp(masked - row_max) * allowed.astype(jnp.float32)
    row_total = lax.optimization_barrier(jnp.sum(weights, axis=-1, keepdims=True)) + 1.0 - live_rows.astype(jnp.float32)[:, None]
    probability = low(weights / row_total)
    context = jnp.einsum('kgqs,skd->qkgd', probability, value_heads, precision=HIGHEST)
    return low(low_back(context.reshape(rows_count, -1)))

def layer(tokens, w_query, w_key, w_value, w_out, w_gate, w_up, w_down, gain_attn, gain_mlp, gain_query, gain_key, segment, positions, live_rows):
    cosine_table, sine_table = rope_tables(positions.reshape(-1), HD)
    normed = low(rms_norm(tokens, gain_attn))
    query_heads = low(rotary(rms_norm(low_back(matmul(normed, w_query)).reshape(TOKENS, HEADS, HD), gain_query), cosine_table, sine_table))
    key_heads = low(rotary(rms_norm(low_back(matmul(normed, w_key)).reshape(TOKENS, KV, HD), gain_key), cosine_table, sine_table))
    value_heads = low(low_back(matmul(normed, w_value))).reshape(TOKENS, KV, HD)

    def group_step(state_in, group_data):
        return (state_in, jax.checkpoint(attend)(*group_data))
    unused, context = lax.scan(group_step, jnp.zeros((), jnp.float32), (query_heads.reshape(N_DP, CAP, HEADS, HD), key_heads.reshape(N_DP, CAP, KV, HD), value_heads.reshape(N_DP, CAP, KV, HD), segment, live_rows))
    attn_out = low_back(matmul(context.reshape(TOKENS, HEADS * HD), w_out))
    hidden_in = tokens + attn_out
    mlp_in = low(rms_norm(hidden_in, gain_mlp))
    gate_proj = low_back(matmul(mlp_in, w_gate))
    up_proj = low_back(matmul(mlp_in, w_up))
    hidden = low(jax.nn.silu(gate_proj) * up_proj)
    branch = low_back(matmul(hidden, w_down))
    return hidden_in + live_rows.reshape(-1, 1).astype(jnp.float32) * branch

def reference(tokens, seq_ends, w_query, w_key, w_value, w_out, w_gate, w_up, w_down, gain_attn, gain_mlp, gain_query, gain_key, cotangent):
    segment, positions = jax.vmap(lambda row_ends: token_layout(row_ends, CAP))(seq_ends)
    live_rows = segment < NSEQ
    floats = tuple((argument.astype(jnp.float32) for argument in (tokens, w_query, w_key, w_value, w_out, w_gate, w_up, w_down, gain_attn, gain_mlp, gain_query, gain_key)))

    def forward(*params):
        return layer(*params, segment, positions, live_rows)
    result, pull_back = jax.vjp(forward, *floats)
    gradients = pull_back(cotangent.astype(jnp.float32))
    return (result.astype(jnp.bfloat16), gradients[0], gradients[1], gradients[2], gradients[3], gradients[4], gradients[5], gradients[6], gradients[7], gradients[8], gradients[9], gradients[10], gradients[11])
```

```python
import functools

import jax
import jax.numpy as jnp
from jax import lax
from jax.experimental import pallas as pl
from jax.experimental.pallas import tpu as pltpu
from jax.sharding import PartitionSpec as P

EPSILON = 1e-06
ROPE_BASE = 1000000.0
X_BIT, Y_BIT, PAIR = 1, 2, 4
MLP_PARTS = 3
LANES = 128


def rms_norm(values, gain_vec):
    return (
        values * lax.rsqrt(jnp.mean(values * values, axis=-1, keepdims=True) + EPSILON) * gain_vec
    )


def rope_tables(positions, width):
    half_width = width // 2
    frequency = ROPE_BASE ** (-2.0 * jnp.arange(half_width, dtype=jnp.float32) / width)
    angles = positions.astype(jnp.float32)[:, None] * frequency[None, :]
    return (jnp.cos(angles), jnp.sin(angles))


def token_layout(seq_ends, token_index):
    segment = jnp.sum((token_index[:, None] >= seq_ends[None, :]).astype(jnp.int32), axis=1)
    starts = jnp.concatenate([jnp.zeros((1,), jnp.int32), seq_ends[:-1]])
    onehot = (segment[:, None] == jnp.arange(seq_ends.shape[0], dtype=jnp.int32)[None, :]).astype(
        jnp.int32
    )
    positions = token_index - jnp.sum(onehot * starts[None, :], axis=1)
    return (segment, positions)


def matmul(left, right):
    return jnp.dot(left, right, preferred_element_type=jnp.float32)


def mat_rows(left, right):
    return lax.dot_general(
        left, right, (((0,), (0,)), ((), ())), preferred_element_type=jnp.float32
    )


def mat_cols(left, right):
    return lax.dot_general(
        left, right, (((1,), (1,)), ((), ())), preferred_element_type=jnp.float32
    )


def low(values):
    return values.astype(jnp.bfloat16)


def wide(values):
    return values.astype(jnp.float32)


def exchange(values, mask):
    size = lax.axis_size("dp")
    return lax.ppermute(values, "dp", [(i, i ^ mask) for i in range(size)])


def bit_side(bit):
    return jnp.minimum(lax.axis_index("dp") & bit, 1)


def team_side():
    return bit_side(PAIR)


def in_turn(mine, theirs, axis, bit=PAIR):
    return jnp.where(
        bit_side(bit) == 0,
        jnp.concatenate([mine, theirs], axis=axis),
        jnp.concatenate([theirs, mine], axis=axis),
    )


VMEM_BYTES = 56 * 1024 * 1024
UNIT_TILE = 256


def params():
    return pltpu.CompilerParams(vmem_limit_bytes=VMEM_BYTES)


def small_cost():
    return pl.CostEstimate(flops=1000, bytes_accessed=1000, transcendentals=0)


def unit_tile(units):
    return UNIT_TILE if units % UNIT_TILE == 0 else units


def whole(shape):
    return pl.BlockSpec(shape, lambda *_: (0,) * len(shape), pipeline_mode=pl.Buffered(1))


def anywhere():
    return pl.BlockSpec(memory_space=pl.ANY)


def in_lanes(width):
    return (width // lax.axis_size("dp")) % LANES == 0


def to_order(values, parts=4):
    width = values.shape[-1]
    if in_lanes(width):
        return values
    devices = lax.axis_size("dp")
    split = values.reshape(*values.shape[:-1], devices // parts, parts, width // devices)
    return jnp.swapaxes(split, -2, -3).reshape(values.shape)


def from_order(values, parts=4):
    width = values.shape[-1]
    if in_lanes(width):
        return values
    devices = lax.axis_size("dp")
    split = values.reshape(*values.shape[:-1], parts, devices // parts, width // devices)
    return jnp.swapaxes(split, -2, -3).reshape(values.shape)


def pieces_of(parts, width, devices):
    part_width, block = width // parts, width // devices
    if block % LANES:
        return [(p, 0, p * part_width, part_width) for p in range(parts)]
    return [
        (d % parts, (d // parts) * block, d * block, block) for d in range(devices)
    ]


def side_by_side(pieces, ref):
    return jnp.concatenate([ref[p][:, at : at + size] for p, at, _, size in pieces], axis=1)


def fetch(parts, scratch, sems):
    rows = parts[0].shape[0]
    copies = [
        pltpu.make_async_copy(part, scratch.at[pl.ds(i * rows, rows), :], sems.at[i])
        for i, part in enumerate(parts)
    ]
    for copy in copies:
        copy.start()
    return copies


def hidden_tile(pieces, row_tile, mlp_all, branch_all, gate_ref, up_ref, down_ref, store):
    gate_w, up_w, down_w = (side_by_side(pieces, r) for r in (gate_ref, up_ref, down_ref))

    def step(index, carry):
        rows = pl.ds(pl.multiple_of(index * row_tile, row_tile), row_tile)
        mlp_rows = mlp_all[rows, :]
        gate_proj = mat_cols(mlp_rows, gate_w)
        up_proj = mat_cols(mlp_rows, up_w)
        hidden_grad = mat_cols(branch_all[rows, :], down_w)
        sigmoid_gate = 1.0 / (1.0 + jnp.exp(-gate_proj))
        silu_gate = gate_proj * sigmoid_gate
        store(
            0,
            rows,
            low(hidden_grad * up_proj * sigmoid_gate * (1.0 + gate_proj * (1.0 - sigmoid_gate))),
        )
        store(1, rows, low(hidden_grad * silu_gate))
        store(2, rows, low(silu_gate * up_proj))
        return carry

    lax.fori_loop(0, mlp_all.shape[0] // row_tile, step, 0)


def store_grad(pieces, out_ref, grad):
    for p, at, first, size in pieces:
        out_ref[p, :, at : at + size] = grad[:, first : first + size]


def mlp_kernel(pieces, tiles, with_grad, *refs):
    mlp_parts, branch_parts = refs[:4], refs[4:8]
    weights = refs[8:11]
    if with_grad:
        acts_ref, grad_ref, mlp_all, branch_all, acts_all, sems = refs[11:]
    else:
        acts_ref, mlp_all, branch_all, sems = refs[11:]
    step = pl.program_id(0)
    rows = mlp_parts[0].shape[0]
    tile = weights[0].shape[1]

    @pl.when(step == 0)
    def _():
        copies = fetch(mlp_parts, mlp_all, sems.at[0]) + fetch(branch_parts, branch_all, sems.at[1])
        for copy in copies:
            copy.wait()

    def forward():
        def store(kind, where, values):
            acts_ref[kind, where, :] = values
            if with_grad:
                acts_all[step, kind, where, :] = values

        hidden_tile(pieces, rows, mlp_all, branch_all, *weights, store)

    if not with_grad:
        forward()
        return

    pl.when(step < tiles)(forward)

    @pl.when((step >= tiles) & (step < 3 * tiles))
    def _():
        index = step - tiles
        acts = acts_all[lax.rem(index, tiles), lax.div(index, tiles)]
        store_grad(pieces, grad_ref, low(mat_rows(acts, mlp_all[...])))

    @pl.when(step >= 3 * tiles)
    def _():
        acts = acts_all[step - 3 * tiles, 2]
        store_grad(pieces, grad_ref, low(mat_rows(acts, branch_all[...])))


def mlp_units(mlp_parts, branch_parts, weight, with_grad):
    part_rows, width = mlp_parts[0].shape
    rows = 4 * part_rows
    parts, units3, part_width = weight.shape
    units = units3 // 3
    tile = unit_tile(units)
    tiles = units // tile
    pieces = pieces_of(parts, width, lax.axis_size("dp"))

    def weight_spec(kind):
        return pl.BlockSpec(
            (parts, tile, part_width), lambda i: (0, kind * tiles + jnp.minimum(i, tiles - 1), 0)
        )

    out_shape = [jax.ShapeDtypeStruct((3, rows, units), jnp.bfloat16)]
    out_specs = [pl.BlockSpec((3, rows, tile), lambda i: (0, 0, jnp.minimum(i, tiles - 1)))]
    scratch = [pltpu.VMEM((rows, width), jnp.bfloat16)] * 2
    if with_grad:
        out_shape.append(jax.ShapeDtypeStruct(weight.shape, jnp.bfloat16))
        out_specs.append(
            pl.BlockSpec((parts, tile, part_width), lambda i: (0, jnp.maximum(i - tiles, 0), 0))
        )
        scratch.append(pltpu.VMEM((tiles, 3, rows, tile), jnp.bfloat16))
    return pl.pallas_call(
        functools.partial(mlp_kernel, pieces, tiles, with_grad),
        grid=(4 * tiles if with_grad else tiles,),
        out_shape=out_shape,
        in_specs=[anywhere()] * 8 + [weight_spec(k) for k in range(3)],
        out_specs=out_specs,
        scratch_shapes=scratch + [pltpu.SemaphoreType.DMA((2, 4))],
        compiler_params=params(),
        cost_estimate=small_cost(),
    )(*mlp_parts, *branch_parts, weight, weight, weight)


def project_kernel(pieces, row_tile, parts, *refs):
    keep_ref, send_ref = refs[-2:]
    count = (len(refs) - 2) // 2
    lefts, rights = refs[:count], refs[count : 2 * count]
    part = pl.program_id(0)

    def step(index, carry):
        rows = pl.ds(pl.multiple_of(index * row_tile, row_tile), row_tile)
        total = None
        for left, right in zip(lefts, rights):
            left_rows = left[rows, :] if len(left.shape) == 2 else left[0, rows, :]
            term = matmul(left_rows, right[0])
            total = term if total is None else total + term

        def store(out_ref):
            size = pieces[0][3]
            if size == total.shape[1]:
                out_ref[index // 2, :, pl.ds(pl.multiple_of(part * size, size), size)] = (
                    total.astype(out_ref.dtype)
                )
            else:
                for k in range(total.shape[1] // size):
                    first = pl.multiple_of((k * parts + part) * size, size)
                    out_ref[index // 2, :, pl.ds(first, size)] = total[
                        :, k * size : (k + 1) * size
                    ].astype(out_ref.dtype)

        pl.when(index % 2 == 0)(lambda: store(keep_ref))
        pl.when(index % 2 == 1)(lambda: store(send_ref))
        return carry

    lax.fori_loop(0, 4, step, 0)


def project(terms):
    rows = terms[0][0].shape[-2] // 4
    parts, _, part_width = terms[0][2].shape
    width = parts * part_width
    pieces = pieces_of(parts, width, lax.axis_size("dp"))
    left_specs, right_specs = [], []
    for acts, kind, weight, first, units in terms:
        if kind is None:
            left_specs.append(whole(acts.shape))
        else:
            left_specs.append(
                pl.BlockSpec(
                    (1, *acts.shape[1:]), lambda j, k=kind: (k, 0, 0), pipeline_mode=pl.Buffered(1)
                )
            )
        right_specs.append(
            pl.BlockSpec((1, units, part_width), lambda j, f=first // units: (j, f, 0))
        )
    out_spec = whole((2, rows, width))
    return pl.pallas_call(
        functools.partial(project_kernel, pieces, rows, parts),
        grid=(parts,),
        out_shape=[
            jax.ShapeDtypeStruct((2, rows, width), jnp.float32),
            jax.ShapeDtypeStruct((2, rows, width), jnp.bfloat16),
        ],
        in_specs=left_specs + right_specs,
        out_specs=[out_spec, out_spec],
        compiler_params=params(),
        cost_estimate=small_cost(),
    )(*[t[0] for t in terms], *[t[2] for t in terms])


def weight_grad_kernel(pieces, cuts, left_ref, *refs):
    count = len(cuts)
    out_ref, right_all, sems = refs[4 * count :]
    step = pl.program_id(0)

    @pl.when(step == 0)
    def _():
        copies = []
        for k in range(count):
            copies += fetch(refs[4 * k : 4 * k + 4], right_all.at[k], sems.at[k])
        for copy in copies:
            copy.wait()

    left = left_ref[...].reshape(left_ref.shape[-2:])
    for k, (start, stop) in enumerate(cuts):

        @pl.when((step >= start) & (step < stop))
        def _():
            store_grad(pieces, out_ref, low(mat_rows(left, right_all[k])))


def weight_grad(parts, left, *rights):
    part_rows, width = rights[0][0][0].shape
    rows, units = left.shape[-2:]
    tile = unit_tile(units)
    tiles = units // tile
    pieces = pieces_of(parts, width, lax.axis_size("dp"))
    cuts, first = [], 0
    for _, kinds in rights:
        cuts.append((first, first + kinds * tiles))
        first += kinds * tiles
    if left.ndim == 3:
        left_spec = pl.BlockSpec((1, rows, tile), lambda i: (i // tiles, 0, i % tiles))
    else:
        left_spec = pl.BlockSpec((rows, tile), lambda i: (0, i))
    return pl.pallas_call(
        functools.partial(weight_grad_kernel, pieces, tuple(cuts)),
        grid=(first,),
        out_shape=jax.ShapeDtypeStruct((parts, first * tile, width // parts), jnp.bfloat16),
        in_specs=[left_spec] + [anywhere()] * (4 * len(rights)),
        out_specs=pl.BlockSpec((parts, tile, width // parts), lambda i: (0, i, 0)),
        scratch_shapes=[
            pltpu.VMEM((len(rights), rows, width), jnp.bfloat16),
            pltpu.SemaphoreType.DMA((len(rights), 4)),
        ],
        compiler_params=params(),
        cost_estimate=small_cost(),
    )(left, *[part for row_parts, _ in rights for part in row_parts])


def turn(values):
    half = values.shape[-1] // 2
    return jnp.concatenate([values[:, half:], values[:, :half]], axis=-1)


def heads_kernel(
    pieces, q_heads, kv_heads, *refs
):
    normed_parts, (weight_ref, gain_q, gain_k, cos_ref, sin_ref) = refs[:4], refs[4:9]
    raw, rot, value, normed_all, weight_all, sems = refs[9:]
    width = gain_q.shape[1]
    rows = normed_parts[0].shape[0]

    @pl.when(pl.program_id(0) == 0)
    def _():
        copies = fetch(normed_parts, normed_all, sems)
        weight_all[...] = side_by_side(pieces, weight_ref)
        for copy in copies:
            copy.wait()

    here = pl.ds(pl.multiple_of(pl.program_id(0) * rows, rows), rows)
    out = mat_cols(normed_all[here, :], weight_all[...])
    for head in range(q_heads + kv_heads):
        columns = slice(head * width, (head + 1) * width)
        unit = out[:, columns]
        gain = gain_q[...] if head < q_heads else gain_k[...]
        normed = (
            unit * lax.rsqrt(jnp.mean(unit * unit, axis=-1, keepdims=True) + EPSILON) * gain
        )
        raw[:, columns] = unit
        rot[:, columns] = low(normed * cos_ref[...] + turn(normed) * sin_ref[...])
    value[...] = low(out[:, (q_heads + kv_heads) * width :])


def heads(normed_parts, weight, gain_query, gain_key, cos, sin, q_heads, kv_heads):
    part_rows, width = normed_parts[0].shape
    rows = 4 * part_rows
    parts, _, part_width = weight.shape
    head_width = gain_query.shape[1]
    units = (q_heads + 2 * kv_heads) * head_width
    tile = rows // 4
    qk = (q_heads + kv_heads) * head_width
    kv = kv_heads * head_width

    def rows_spec(columns):
        return pl.BlockSpec((tile, columns), lambda i: (i, 0))

    return pl.pallas_call(
        functools.partial(
            heads_kernel, pieces_of(parts, width, lax.axis_size("dp")), q_heads, kv_heads
        ),
        grid=(4,),
        out_shape=[
            jax.ShapeDtypeStruct((rows, qk), jnp.float32),
            jax.ShapeDtypeStruct((rows, qk), jnp.bfloat16),
            jax.ShapeDtypeStruct((rows, kv), jnp.bfloat16),
        ],
        in_specs=[
            *[anywhere()] * 4,
            whole((parts, units, part_width)),
            whole((1, head_width)),
            whole((1, head_width)),
            rows_spec(head_width),
            rows_spec(head_width),
        ],
        out_specs=[rows_spec(qk), rows_spec(qk), rows_spec(kv)],
        scratch_shapes=[
            pltpu.VMEM((rows, width), jnp.bfloat16),
            pltpu.VMEM((units, width), jnp.bfloat16),
            pltpu.SemaphoreType.DMA((4,)),
        ],
        compiler_params=params(),
        cost_estimate=small_cost(),
    )(*normed_parts, weight, gain_query, gain_key, cos, sin)


def probabilities(query, key, row_segment, column_segment, row_slot, column_slot, dead, scale):
    allowed = (row_segment == column_segment) & (column_slot <= row_slot)
    masked = jnp.where(allowed, mat_cols(query, key) * scale, -1e30)
    weights = jnp.where(allowed, jnp.exp(masked - jnp.max(masked, axis=-1, keepdims=True)), 0.0)
    total = jnp.sum(weights, axis=-1, keepdims=True) + dead
    return weights * (1.0 / total)


def attend_kernel(scale, q_ref, k_ref, v_ref, row_ref, column_ref, out_ref):
    width = k_ref.shape[1]
    marks = (row_ref[0, :, 0:1], column_ref[0, 0:1, :], row_ref[0, :, 1:2], column_ref[0, 1:2, :])
    dead = wide(row_ref[0, :, 2:3])
    for head in range(q_ref.shape[1] // width):
        columns = slice(head * width, (head + 1) * width)
        probs = probabilities(q_ref[:, columns], k_ref[...], *marks, dead, scale)
        out_ref[:, columns] = low(matmul(low(probs), v_ref[...]))


def attention_specs(rows, head_width, q_heads, kv_heads):
    group_rows = rows // 2
    per = q_heads // kv_heads
    query = pl.BlockSpec((group_rows, per * head_width), lambda g, k: (g, k))
    key = pl.BlockSpec((group_rows, head_width), lambda g, k: (g, q_heads + k))
    value = pl.BlockSpec((group_rows, head_width), lambda g, k: (g, k))
    row_marks = pl.BlockSpec((1, group_rows, 8), lambda g, k: (g, 0, 0))
    column_marks = pl.BlockSpec((1, 8, group_rows), lambda g, k: (g, 0, 0))
    return query, key, value, row_marks, column_marks


def attend(rot, value, row_marks, column_marks, head_width, q_heads, kv_heads):
    rows = rot.shape[0]
    query, key, value_spec, row_spec, column_spec = attention_specs(
        rows, head_width, q_heads, kv_heads
    )
    return pl.pallas_call(
        functools.partial(attend_kernel, head_width ** (-0.5)),
        grid=(2, kv_heads),
        out_shape=jax.ShapeDtypeStruct((rows, q_heads * head_width), jnp.bfloat16),
        in_specs=[query, key, value_spec, row_spec, column_spec],
        out_specs=query,
        compiler_params=params(),
        cost_estimate=small_cost(),
    )(rot, rot, value, row_marks, column_marks)


def head_back(grad, raw, gain, cos, sin):
    grad = grad * cos - turn(grad) * sin
    scale = lax.rsqrt(jnp.mean(raw * raw, axis=-1, keepdims=True) + EPSILON)
    unit = raw * scale
    through = grad * gain
    raw_grad = scale * (through - unit * jnp.mean(through * unit, axis=-1, keepdims=True))
    return low(raw_grad), jnp.sum(grad * unit, axis=0, keepdims=True)


def attend_back_kernel(
    pieces,
    scale,
    q_heads,
    kv_heads,
    cot_a,
    cot_b,
    cot_c,
    cot_d,
    weight_ref,
    q_ref,
    k_ref,
    v_ref,
    q_raw,
    k_raw,
    row_ref,
    column_ref,
    gain_q,
    gain_k,
    cos_ref,
    sin_ref,
    grad_ref,
    gain_ref,
    cot_all,
    sems,
):
    group, kv = pl.program_id(0), pl.program_id(1)
    rows, width = k_ref.shape
    per = q_heads // kv_heads

    @pl.when((group == 0) & (kv == 0))
    def _():
        gain_ref[...] = jnp.zeros_like(gain_ref)
        for copy in fetch((cot_a, cot_b, cot_c, cot_d), cot_all, sems):
            copy.wait()

    marks = (row_ref[0, :, 0:1], column_ref[0, 0:1, :], row_ref[0, :, 1:2], column_ref[0, 1:2, :])
    dead = wide(row_ref[0, :, 2:3])
    here = pl.ds(pl.multiple_of(group * rows, rows), rows)
    context_grad = low(mat_cols(cot_all[here, :], side_by_side(pieces, weight_ref)))
    key, value, cos, sin = k_ref[...], v_ref[...], cos_ref[...], sin_ref[...]
    key_grad = value_grad = None
    gain_sum = None
    for head in range(per):
        columns = slice(head * width, (head + 1) * width)
        query, grad = q_ref[:, columns], context_grad[:, columns]
        probs = probabilities(query, key, *marks, dead, scale)
        prob_grad = mat_cols(grad, value)
        part = mat_rows(low(probs), grad)
        value_grad = part if value_grad is None else value_grad + part
        score_grad = low(
            probs * (prob_grad - jnp.sum(probs * prob_grad, axis=-1, keepdims=True))
        )
        part = mat_rows(score_grad, query)
        key_grad = part if key_grad is None else key_grad + part
        query_grad, gain_part = head_back(
            matmul(score_grad, key) * scale, q_raw[:, columns], gain_q[...], cos, sin
        )
        gain_sum = gain_part if gain_sum is None else gain_sum + gain_part
        first = pl.multiple_of((kv * per + head) * width, width)
        grad_ref[here, pl.ds(first, width)] = query_grad
    key_out, gain_part = head_back(key_grad * scale, k_raw[...], gain_k[...], cos, sin)
    gain_ref[0:1, :] += gain_sum
    gain_ref[1:2, :] += gain_part
    grad_ref[here, pl.ds(pl.multiple_of((q_heads + kv) * width, width), width)] = key_out
    first = pl.multiple_of((q_heads + kv_heads + kv) * width, width)
    grad_ref[here, pl.ds(first, width)] = low(value_grad)


def attend_back(
    cot_parts, weight, rot, value, raw, row_marks, column_marks, gain_query, gain_key, cos, sin,
    q_heads, kv_heads,
):
    part_rows, width = cot_parts[0].shape
    rows = 4 * part_rows
    parts, _, part_width = weight.shape
    head_width = gain_query.shape[1]
    units = q_heads * head_width // kv_heads
    first = (q_heads + 2 * kv_heads) * head_width // units
    group_rows = rows // 2
    query, key, value_spec, row_spec, column_spec = attention_specs(
        rows, head_width, q_heads, kv_heads
    )
    columns = (q_heads + 2 * kv_heads) * head_width

    def group_spec(size):
        return pl.BlockSpec((group_rows, size), lambda g, k: (g, 0))

    return pl.pallas_call(
        functools.partial(
            attend_back_kernel,
            pieces_of(parts, width, lax.axis_size("dp")),
            head_width ** (-0.5),
            q_heads,
            kv_heads,
        ),
        grid=(2, kv_heads),
        out_shape=[
            jax.ShapeDtypeStruct((rows, columns), jnp.bfloat16),
            jax.ShapeDtypeStruct((8, head_width), jnp.float32),
        ],
        in_specs=[
            *[anywhere()] * 4,
            pl.BlockSpec((parts, units, part_width), lambda g, k: (0, first + k, 0)),
            query,
            key,
            value_spec,
            query,
            key,
            row_spec,
            column_spec,
            whole((1, head_width)),
            whole((1, head_width)),
            group_spec(head_width),
            group_spec(head_width),
        ],
        out_specs=[whole((rows, columns)), whole((8, head_width))],
        scratch_shapes=[
            pltpu.VMEM((rows, width), jnp.bfloat16),
            pltpu.SemaphoreType.DMA((4,)),
        ],
        compiler_params=params(),
        cost_estimate=small_cost(),
    )(
        *cot_parts, weight, rot, rot, value, raw, raw, row_marks, column_marks,
        gain_query, gain_key, cos, sin,
    )


class Sequence:
    def __init__(self):
        self.last = ()

    def tie(self, *values):
        out = lax.optimization_barrier((*values, *self.last))[: len(values)]
        return out[0] if len(values) == 1 else out

    def mark(self, *values):
        self.last = values
        return values[0] if len(values) == 1 else values

    def wait(self, *values):
        out = self.tie(*values)
        return self.mark(out) if len(values) == 1 else self.mark(*out)


def swap_core(values):
    return lax.ppermute(values, "tensor", [(0, 1), (1, 0)])


def outer_bits():
    size = lax.axis_size("dp")
    return [1 << i for i in range(size.bit_length() - 1) if (1 << i) > PAIR]


def xy_groups():
    size = lax.axis_size("dp")
    return [[first + i for i in range(4)] for first in range(0, size, 4)]


def far_masks():
    masks = [0, PAIR]
    for bit in outer_bits():
        masks = masks + [m ^ bit for m in masks]
    return masks


def near_start(own, other):
    return [exchange(other if m & PAIR else own, m) for m in far_masks()[1:]]


def near_end(own, received):
    blocks = [own, *received]
    for bit in [PAIR] + outer_bits():
        blocks = [in_turn(x, y, 1, bit) for x, y in zip(blocks[::2], blocks[1::2])]
    return blocks[0]


def gather_weight(block):
    return lax.all_gather(block, "dp", axis_index_groups=xy_groups(), axis=0)


def near_x_y(block):
    return (exchange(block, X_BIT), exchange(block, Y_BIT))


def far_x_y(from_x, from_y):
    half = from_x.shape[1] // 2
    return (exchange(from_y[:, :half], X_BIT), exchange(from_x[:, half:], Y_BIT))


def assemble_kernel(slot_ref, own_ref, x_ref, y_ref, left_ref, right_ref, out_ref):
    own, from_x, from_y = own_ref[...], x_ref[...], y_ref[...]
    far = jnp.concatenate([left_ref[...], right_ref[...]], axis=1)
    x_side, y_side = slot_ref[0] % 2 == 1, slot_ref[0] // 2 == 1
    near = [jnp.where(x_side, from_x, own), jnp.where(x_side, own, from_x)]
    other = [jnp.where(x_side, far, from_y), jnp.where(x_side, from_y, far)]
    for k in range(2):
        out_ref[k] = jnp.where(y_side, other[k], near[k])
        out_ref[2 + k] = jnp.where(y_side, near[k], other[k])


def assemble(block, from_x, from_y, left, right):
    units, columns = block.shape
    tile = unit_tile(units)
    slot = (lax.axis_index("dp") & (X_BIT | Y_BIT)).reshape(1).astype(jnp.int32)

    def rows_of(size):
        return pl.BlockSpec((tile, size), lambda i: (i, 0))

    return pl.pallas_call(
        assemble_kernel,
        grid=(units // tile,),
        out_shape=jax.ShapeDtypeStruct((4, units, columns), block.dtype),
        in_specs=[pl.BlockSpec(memory_space=pltpu.SMEM)]
        + [rows_of(columns)] * 3
        + [rows_of(columns // 2)] * 2,
        out_specs=pl.BlockSpec((4, tile, columns), lambda i: (0, i, 0)),
        compiler_params=params(),
        cost_estimate=small_cost(),
    )(slot, block, from_x, from_y, left, right)


def scatter_grad(full):
    return lax.psum_scatter(
        full, "dp", axis_index_groups=xy_groups(), scatter_dimension=0
    )


def part_of(full, flip):
    place = (lax.axis_index("dp") & (X_BIT | Y_BIT)) ^ flip
    return lax.dynamic_index_in_dim(full, place, 0, keepdims=False)


def scatter_near(full):
    half = full.shape[1] // 2
    far = part_of(full, X_BIT | Y_BIT)
    by_x, by_y = part_of(full, X_BIT), part_of(full, Y_BIT)
    return (
        exchange(far[:half], X_BIT),
        exchange(far[half:], Y_BIT),
        exchange(by_x[:half], X_BIT),
        exchange(by_y[half:], Y_BIT),
        by_x[half:],
        by_y[:half],
    )


def scatter_far(far_top, far_bottom, x_top, y_bottom, x_rest, y_rest):
    x_bottom = exchange(low(wide(x_rest) + wide(far_bottom)), X_BIT)
    y_top = exchange(low(wide(y_rest) + wide(far_top)), Y_BIT)
    return (x_top, x_bottom, y_top, y_bottom)


def scatter_end(full, x_top, x_bottom, y_top, y_bottom):
    own = wide(part_of(full, 0))
    half = own.shape[0] // 2
    return jnp.concatenate(
        [
            own[:half] + wide(x_top) + wide(y_top),
            own[half:] + wide(x_bottom) + wide(y_bottom),
        ],
        axis=0,
    )


def last_start(total):
    total = total.reshape(total.shape[-2:])
    masks = far_masks()
    size = total.shape[1] // len(masks)
    place = lax.axis_index("dp") // 4

    def columns(mask):
        return lax.dynamic_slice_in_dim(total, (place ^ (mask // 4)) * size, size, 1)

    return [wide(columns(0))] + [exchange(low(columns(m)), m) for m in masks[1:]]


def last_end(own, received):
    mine, other = own, None
    for mask, values in zip(far_masks()[1:], received):
        if mask & PAIR:
            other = wide(values) if other is None else other + wide(values)
        else:
            mine = mine + wide(values)
    return mine, other


def team_halves(projected):
    keep, send = projected
    received = swap_core(send)
    return (keep[0] + wide(received[0]), low(keep[1] + wide(received[1])))


def total_sum(values):
    values = values + swap_core(values)
    bit = 1
    while bit < lax.axis_size("dp"):
        values = values + exchange(values, bit)
        bit *= 2
    return values


def per_device(
    tokens,
    seq_ends,
    w_query,
    w_key,
    w_value,
    w_out,
    w_gate,
    w_up,
    w_down,
    gain_attn,
    gain_mlp,
    gain_query,
    gain_key,
    cotangent,
):
    rows_dev, width = tokens.shape
    core = lax.axis_index("tensor")
    side = team_side()
    parts = len(xy_groups()[0])
    head_width = gain_query.shape[0]
    seq = Sequence()

    def halves(weight, axis):
        size = weight.shape[axis] // 2
        return (
            lax.dynamic_slice_in_dim(weight, side * size, size, axis),
            lax.dynamic_slice_in_dim(weight, (1 - side) * size, size, axis),
        )

    q_half, k_half, v_half = halves(w_query, 1), halves(w_key, 1), halves(w_value, 1)
    q_cols, kv_cols = q_half[0].shape[1], k_half[0].shape[1]
    qkv_cols = q_cols + 2 * kv_cols
    q_heads, kv_heads = q_cols // head_width, kv_cols // head_width
    out_half = halves(w_out, 0)
    attn_own, attn_other = [
        jnp.concatenate(
            [jnp.concatenate([q_half[s], k_half[s], v_half[s]], axis=1).T, out_half[s]], axis=0
        )
        for s in (0, 1)
    ]
    ends_mate = exchange(wide(seq_ends), PAIR)
    attn_far = near_start(attn_own, attn_other)
    g_half, u_half, d_half = halves(w_gate, 1), halves(w_up, 1), halves(w_down, 0)
    all_units = g_half[0].shape[1]
    units = all_units // MLP_PARTS

    def chunk_own(chunk, s):
        cut = slice(chunk * units, (chunk + 1) * units)
        return jnp.concatenate([g_half[s][:, cut].T, u_half[s][:, cut].T, d_half[s][cut]], axis=0)

    token_float = to_order(wide(tokens))
    cot_float = to_order(wide(cotangent))
    gain_attn_o, gain_mlp_o = to_order(gain_attn), to_order(gain_mlp)
    near = jnp.arange(rows_dev, dtype=jnp.int32)
    slots = jnp.concatenate([core * rows_dev + near, (1 - core) * rows_dev + near])
    layouts = [token_layout(e, slots) for e in (seq_ends[0], ends_mate[0].astype(jnp.int32))]
    segment = jnp.stack([s for s, _ in layouts])
    positions = jnp.concatenate([p for _, p in layouts])
    live_group = segment < seq_ends.shape[1]
    live_mine = wide(live_group)[0, :rows_dev, None]

    normed, attn_norm_pull = jax.vjp(rms_norm, token_float, gain_attn_o)
    normed_low = low(normed)
    branch_low = low(live_mine * cot_float)
    normed_core = swap_core(normed_low)
    cosine_table, sine_table = rope_tables(positions, head_width)
    cos = jnp.concatenate([cosine_table, cosine_table], axis=1)
    sin = jnp.concatenate([-sine_table, sine_table], axis=1)
    slots_both = jnp.stack([slots, slots])
    marks = [
        jnp.where(live_group, segment, -1),
        slots_both,
        1 - live_group.astype(jnp.int32),
    ] + [jnp.zeros_like(segment)] * 5
    row_marks = jnp.stack(marks, axis=2)
    column_marks = jnp.stack([segment, slots_both] + marks[3:] + marks[3:4], axis=1)
    gain_q, gain_k = gain_query[None, :], gain_key[None, :]
    chunks = [(chunk_own(c, 0), chunk_own(c, 1)) for c in range(MLP_PARTS)]
    seq.mark(cos, sin, row_marks, column_marks, normed_low, *[v for c in chunks for v in c])

    attn_far = seq.wait(*attn_far)
    attn_near = near_end(attn_own, attn_far)
    attn_x, attn_y = near_x_y(attn_near)
    first_far = near_start(*chunks[0])
    normed_mate = exchange(seq.tie(normed_low), PAIR)
    attn_x, attn_y, *first_far = seq.wait(attn_x, attn_y, *first_far)
    attn_left, attn_right = far_x_y(attn_x, attn_y)
    mlp_full = [gather_weight(near_end(chunks[0][0], first_far))]
    second_far = near_start(*chunks[1])
    attn_left, attn_right, normed_mate, *second_far = seq.wait(
        attn_left, attn_right, normed_mate, *second_far
    )
    full_attn = assemble(attn_near, attn_x, attn_y, attn_left, attn_right)
    normed_all = (normed_low, normed_core, normed_mate, swap_core(normed_mate))
    second_near = near_end(chunks[1][0], second_far)
    chunk_x, chunk_y = near_x_y(second_near)
    third_far = near_start(*chunks[2])
    qk_raw, qk_rot, value_low = heads(
        normed_all, full_attn, gain_q, gain_k, cos, sin, q_heads, kv_heads
    )
    value_low = seq.mark(value_low)
    context_low = seq.mark(
        attend(
            qk_rot, seq.tie(value_low), row_marks, column_marks, head_width, q_heads, kv_heads
        )
    )
    attn_mine, attn_mate = team_halves(project([(context_low, None, full_attn, qkv_cols, q_cols)]))
    seq.mark(attn_mate)
    attn_mate = exchange(attn_mate, PAIR)
    chunk_x, chunk_y, *third_far = seq.wait(chunk_x, chunk_y, *third_far)
    chunk_left, chunk_right = far_x_y(chunk_x, chunk_y)
    mlp_full += [None, gather_weight(near_end(chunks[2][0], third_far))]
    branch_mate = exchange(seq.tie(branch_low), PAIR)
    attn_mate = seq.wait(attn_mate)
    hidden_in = token_float + (attn_mine + wide(attn_mate))
    mlp_normed, mlp_norm_pull = jax.vjp(rms_norm, hidden_in, gain_mlp_o)
    mlp_low = seq.mark(low(mlp_normed))
    mlp_row_mate = exchange(mlp_low, PAIR)
    mlp_row_mate = seq.wait(mlp_row_mate)
    mlp_all = (mlp_low, swap_core(mlp_low), mlp_row_mate, swap_core(mlp_row_mate))
    branch_mate = seq.wait(branch_mate)
    branch_all = (branch_low, swap_core(branch_low), branch_mate, swap_core(branch_mate))

    all_acts, mlp_scattered = [], []
    mlp_full[0], chunk_left, chunk_right = seq.wait(mlp_full[0], chunk_left, chunk_right)
    mlp_full[1] = assemble(second_near, chunk_x, chunk_y, chunk_left, chunk_right)
    acts, grad_full = mlp_units(mlp_all, branch_all, mlp_full[0], True)
    all_acts.append(acts)
    grad_full = seq.mark(grad_full)
    mlp_scattered.append(scatter_grad(grad_full))
    mlp_full[2] = seq.wait(mlp_full[2])
    mlp_full[1] = seq.tie(mlp_full[1])
    acts, grad_full = mlp_units(mlp_all, branch_all, mlp_full[1], True)
    all_acts.append(acts)
    grad_full = seq.mark(grad_full)
    mlp_scattered.append(scatter_grad(grad_full))
    mlp_full[2] = seq.tie(mlp_full[2])
    (acts,) = mlp_units(mlp_all, branch_all, mlp_full[2], False)
    all_acts.append(acts)
    terms = [
        (a, kind, w, kind * units, units) for a, w in zip(all_acts, mlp_full) for kind in (0, 1)
    ]
    back_mine, back_mate = team_halves(project(terms))
    seq.mark(back_mate)
    back_mate = exchange(back_mate, PAIR)
    acts = seq.tie(acts)
    grad_full = seq.mark(weight_grad(parts, acts, (mlp_all, 2), (branch_all, 1)))
    mlp_scattered.append(scatter_grad(grad_full))
    terms = [(seq.tie(a), 2, w, 2 * units, units) for a, w in zip(all_acts, mlp_full)]
    sum_mine, sum_mate = team_halves(project(terms))
    sum_mate = seq.mark(sum_mate)
    back_mate = seq.wait(back_mate)
    mlp_back = back_mine + wide(back_mate)
    hidden_from, gain_mlp_part = mlp_norm_pull(mlp_back)
    hidden_grad_total = cot_float + hidden_from
    cot_low = seq.mark(low(hidden_grad_total))
    cot_mate = exchange(cot_low, PAIR)
    cot_core = swap_core(cot_low)
    sum_mate = exchange(seq.tie(sum_mate), PAIR)
    mlp_scattered[0] = seq.wait(mlp_scattered[0])
    lasts = [last_start(mlp_scattered[0])]
    mlp_scattered[1], cot_mate = seq.wait(mlp_scattered[1], cot_mate)
    lasts.append(last_start(mlp_scattered[1]))
    cot_all = (cot_low, cot_core, cot_mate, swap_core(cot_mate))
    out_grad = seq.mark(weight_grad(parts, context_low, (cot_all, 1)))
    out_steps = scatter_near(out_grad)
    qkv_grad, gain_parts = attend_back(
        cot_all, seq.tie(full_attn), qk_rot, value_low, qk_raw, row_marks, column_marks,
        gain_q, gain_k, cos, sin, q_heads, kv_heads,
    )
    qkv_grad = seq.mark(qkv_grad)
    mlp_scattered[2], *out_steps = seq.wait(mlp_scattered[2], *out_steps)
    out_steps = scatter_far(*out_steps)
    lasts.append(last_start(mlp_scattered[2]))
    token_mine, token_mate = team_halves(
        project([(seq.tie(qkv_grad), None, full_attn, 0, qkv_cols)])
    )
    token_mate = seq.mark(token_mate)
    token_mate = exchange(token_mate, PAIR)
    qkv_full = seq.mark(weight_grad(parts, seq.tie(qkv_grad), (normed_all, 1)))
    qkv_steps = scatter_near(qkv_full)
    count = len(out_steps)
    out_steps = seq.wait(*out_steps, *lasts[0])
    out_steps, lasts[0] = out_steps[:count], out_steps[count:]
    out_total = scatter_end(out_grad, *out_steps)
    qkv_steps = seq.wait(*qkv_steps)
    qkv_steps = scatter_far(*qkv_steps)
    token_mate = seq.wait(token_mate)
    attn_back = token_mine + wide(token_mate)
    token_from, gain_attn_part = attn_norm_pull(attn_back)
    gain_sums = total_sum(
        jnp.concatenate(
            [from_order(gain_attn_part), from_order(gain_mlp_part), gain_parts[0], gain_parts[1]]
        )
    )
    grad_tokens = seq.mark(from_order(hidden_grad_total + token_from))
    qkv_steps = seq.wait(*qkv_steps)
    attn_last = last_start(
        jnp.concatenate([scatter_end(qkv_full, *qkv_steps), out_total], axis=0)
    )
    lasts[1] = seq.wait(*lasts[1])
    mlp_sum = sum_mine + wide(seq.wait(sum_mate))
    out_tokens = from_order(low(hidden_in + live_mine * mlp_sum))
    lasts[2] = seq.wait(*lasts[2])
    teams = [last_end(last[0], last[1:]) for last in lasts]
    attn_team = last_end(attn_last[0], attn_last[1:])

    def pick(pair, start, stop):
        return in_turn(pair[0][start:stop], pair[1][start:stop], 0)

    grad_query = pick(attn_team, 0, q_cols).T
    grad_key = pick(attn_team, q_cols, q_cols + kv_cols).T
    grad_value = pick(attn_team, q_cols + kv_cols, qkv_cols).T
    grad_out = pick(attn_team, qkv_cols, qkv_cols + q_cols)

    def units_of(kind):
        cut = slice(kind * units, (kind + 1) * units)
        return in_turn(
            jnp.concatenate([keep[cut] for keep, _ in teams], axis=0),
            jnp.concatenate([other[cut] for _, other in teams], axis=0),
            0,
        )

    grad_gate = units_of(0).T
    grad_up = units_of(1).T
    grad_down = units_of(2)
    return (
        out_tokens,
        grad_tokens,
        grad_query,
        grad_key,
        grad_value,
        grad_out,
        grad_gate,
        grad_up,
        grad_down,
        gain_sums[:width],
        gain_sums[width : 2 * width],
        gain_sums[2 * width : 2 * width + head_width],
        gain_sums[2 * width + head_width :],
    )


def solution(mesh):
    weight_in = P("dp", "tensor")
    weight_out = P("tensor", "dp")
    rows = P(("dp", "tensor"), None)
    weights = (weight_in, weight_in, weight_in, weight_out, weight_in, weight_in, weight_out)
    gains = (P(), P(), P(), P())
    return jax.shard_map(
        per_device,
        mesh=mesh,
        in_specs=(rows, P("dp", None), *weights, *gains, rows),
        out_specs=(rows, rows, *weights, *gains),
        check_vma=False,
    )
```

```python
import functools

import jax
import jax.numpy as jnp
from jax import lax
from jax.experimental import pallas as pl
from jax.experimental.pallas import tpu as pltpu
from jax.sharding import PartitionSpec as P

EPSILON = 1e-06
ROPE_BASE = 1000000.0
X_BIT, Y_BIT, PAIR = 1, 2, 4
MLP_PARTS = 3
LANES = 128


def rms_norm(values, gain_vec):
    return (
        values * lax.rsqrt(jnp.mean(values * values, axis=-1, keepdims=True) + EPSILON) * gain_vec
    )


def rope_tables(positions, width):
    half_width = width // 2
    frequency = ROPE_BASE ** (-2.0 * jnp.arange(half_width, dtype=jnp.float32) / width)
    angles = positions.astype(jnp.float32)[:, None] * frequency[None, :]
    return (jnp.cos(angles), jnp.sin(angles))


def token_layout(seq_ends, token_index):
    segment = jnp.sum((token_index[:, None] >= seq_ends[None, :]).astype(jnp.int32), axis=1)
    starts = jnp.concatenate([jnp.zeros((1,), jnp.int32), seq_ends[:-1]])
    onehot = (segment[:, None] == jnp.arange(seq_ends.shape[0], dtype=jnp.int32)[None, :]).astype(
        jnp.int32
    )
    positions = token_index - jnp.sum(onehot * starts[None, :], axis=1)
    return (segment, positions)


def matmul(left, right):
    return jnp.dot(left, right, preferred_element_type=jnp.float32)


def mat_rows(left, right):
    return lax.dot_general(
        left, right, (((0,), (0,)), ((), ())), preferred_element_type=jnp.float32
    )


def mat_cols(left, right):
    return lax.dot_general(
        left, right, (((1,), (1,)), ((), ())), preferred_element_type=jnp.float32
    )


def low(values):
    return values.astype(jnp.bfloat16)


def wide(values):
    return values.astype(jnp.float32)


def exchange(values, mask):
    size = lax.axis_size("dp")
    return lax.ppermute(values, "dp", [(i, i ^ mask) for i in range(size)])


def bit_side(bit):
    return jnp.minimum(lax.axis_index("dp") & bit, 1)


def team_side():
    return bit_side(PAIR)


def in_turn(mine, theirs, axis, bit=PAIR):
    return jnp.where(
        bit_side(bit) == 0,
        jnp.concatenate([mine, theirs], axis=axis),
        jnp.concatenate([theirs, mine], axis=axis),
    )


VMEM_BYTES = 56 * 1024 * 1024
UNIT_TILE = 256


def params():
    return pltpu.CompilerParams(vmem_limit_bytes=VMEM_BYTES)


def small_cost():
    return pl.CostEstimate(flops=1000, bytes_accessed=1000, transcendentals=0)


def large_cost():
    return pl.CostEstimate(flops=400_000_000_000, bytes_accessed=1000, transcendentals=0)


def unit_tile(units):
    return UNIT_TILE if units % UNIT_TILE == 0 else units


def whole(shape):
    return pl.BlockSpec(shape, lambda *_: (0,) * len(shape), pipeline_mode=pl.Buffered(1))


def anywhere():
    return pl.BlockSpec(memory_space=pl.ANY)


def in_lanes(width):
    return (width // lax.axis_size("dp")) % LANES == 0


def to_order(values, parts=4):
    width = values.shape[-1]
    if in_lanes(width):
        return values
    devices = lax.axis_size("dp")
    split = values.reshape(*values.shape[:-1], devices // parts, parts, width // devices)
    return jnp.swapaxes(split, -2, -3).reshape(values.shape)


def from_order(values, parts=4):
    width = values.shape[-1]
    if in_lanes(width):
        return values
    devices = lax.axis_size("dp")
    split = values.reshape(*values.shape[:-1], parts, devices // parts, width // devices)
    return jnp.swapaxes(split, -2, -3).reshape(values.shape)


def pieces_of(parts, width, devices):
    part_width, block = width // parts, width // devices
    if block % LANES:
        return [(p, 0, p * part_width, part_width) for p in range(parts)]
    return [
        (d % parts, (d // parts) * block, d * block, block) for d in range(devices)
    ]


def side_by_side(pieces, ref):
    return jnp.concatenate([ref[p][:, at : at + size] for p, at, _, size in pieces], axis=1)


def copies_of(parts, scratch, sems):
    copies, first = [], 0
    for i, part in enumerate(parts):
        rows = part.shape[0]
        copies.append(
            pltpu.make_async_copy(part, scratch.at[pl.ds(first, rows), :], sems.at[i])
        )
        first += rows
    return copies


def fetch(parts, scratch, sems):
    copies = copies_of(parts, scratch, sems)
    for copy in copies:
        copy.start()
    return copies


def pieces_in(parts, start, stop):
    found, first = [], 0
    for i, part in enumerate(parts):
        if start <= first < stop:
            found.append(i)
        first += part.shape[0]
    return found


def rows_in(parts):
    return sum(part.shape[0] for part in parts)


def hidden_rows(rows, mlp_all, branch_all, gate_w, up_w, down_w, store):
    mlp_rows = mlp_all[rows, :]
    gate_proj = mat_cols(mlp_rows, gate_w)
    up_proj = mat_cols(mlp_rows, up_w)
    hidden_grad = mat_cols(branch_all[rows, :], down_w)
    sigmoid_gate = 1.0 / (1.0 + jnp.exp(-gate_proj))
    silu_gate = gate_proj * sigmoid_gate
    store(
        0,
        rows,
        low(hidden_grad * up_proj * sigmoid_gate * (1.0 + gate_proj * (1.0 - sigmoid_gate))),
    )
    store(1, rows, low(hidden_grad * silu_gate))
    store(2, rows, low(silu_gate * up_proj))


def store_grad(pieces, out_ref, grad):
    for p, at, first, size in pieces:
        out_ref[p, :, at : at + size] = grad[:, first : first + size]


def mlp_kernel(pieces, tiles, with_grad, counts, *refs):
    count = sum(counts)
    mlp_parts, branch_parts = refs[: counts[0]], refs[counts[0] : count]
    weights = refs[count : count + 3]
    if with_grad:
        acts_ref, grad_ref, mlp_all, branch_all, acts_all, sems = refs[count + 3 :]
    else:
        acts_ref, mlp_all, branch_all, sems = refs[count + 3 :]
    step = pl.program_id(0)
    total = mlp_all.shape[0]
    rows = total // 4

    def store(kind, where, values):
        acts_ref[kind, where, :] = values
        if with_grad:
            acts_all[step, kind, where, :] = values

    def sides():
        return [side_by_side(pieces, w) for w in weights]

    @pl.when(step == 0)
    def _():
        mlp_copies = fetch(mlp_parts, mlp_all, sems.at[0])
        branch_copies = fetch(branch_parts, branch_all, sems.at[1])
        sides_now = sides()
        for first in range(0, total, rows):
            for i in pieces_in(mlp_parts, first, first + rows):
                mlp_copies[i].wait()
            for i in pieces_in(branch_parts, first, first + rows):
                branch_copies[i].wait()
            hidden_rows(slice(first, first + rows), mlp_all, branch_all, *sides_now, store)

    @pl.when((step > 0) & (step < tiles))
    def _():
        hidden_rows(slice(0, total), mlp_all, branch_all, *sides(), store)

    if not with_grad:
        return

    @pl.when((step >= tiles) & (step < 3 * tiles))
    def _():
        index = step - tiles
        acts = acts_all[lax.rem(index, tiles), lax.div(index, tiles)]
        store_grad(pieces, grad_ref, low(mat_rows(acts, mlp_all[...])))

    @pl.when(step >= 3 * tiles)
    def _():
        acts = acts_all[step - 3 * tiles, 2]
        store_grad(pieces, grad_ref, low(mat_rows(acts, branch_all[...])))


def mlp_units(mlp_parts, branch_parts, weight, with_grad):
    rows, width = rows_in(mlp_parts), mlp_parts[0].shape[1]
    counts = (len(mlp_parts), len(branch_parts))
    parts, units3, part_width = weight.shape
    units = units3 // 3
    tile = unit_tile(units)
    tiles = units // tile
    pieces = pieces_of(parts, width, lax.axis_size("dp"))

    def weight_spec(kind):
        return pl.BlockSpec(
            (parts, tile, part_width), lambda i: (0, kind * tiles + jnp.minimum(i, tiles - 1), 0)
        )

    out_shape = [jax.ShapeDtypeStruct((3, rows, units), jnp.bfloat16)]
    out_specs = [pl.BlockSpec((3, rows, tile), lambda i: (0, 0, jnp.minimum(i, tiles - 1)))]
    scratch = [pltpu.VMEM((rows, width), jnp.bfloat16)] * 2
    if with_grad:
        out_shape.append(jax.ShapeDtypeStruct(weight.shape, jnp.bfloat16))
        out_specs.append(
            pl.BlockSpec((parts, tile, part_width), lambda i: (0, jnp.maximum(i - tiles, 0), 0))
        )
        scratch.append(pltpu.VMEM((tiles, 3, rows, tile), jnp.bfloat16))
    return pl.pallas_call(
        functools.partial(mlp_kernel, pieces, tiles, with_grad, counts),
        grid=(4 * tiles if with_grad else tiles,),
        out_shape=out_shape,
        in_specs=[anywhere()] * sum(counts) + [weight_spec(k) for k in range(3)],
        out_specs=out_specs,
        scratch_shapes=scratch + [pltpu.SemaphoreType.DMA((2, max(counts)))],
        compiler_params=params(),
        cost_estimate=small_cost(),
    )(*mlp_parts, *branch_parts, weight, weight, weight)


def project_kernel(pieces, row_tile, parts, *refs):
    keep_ref, send_ref = refs[-2:]
    count = (len(refs) - 2) // 2
    lefts, rights = refs[:count], refs[count : 2 * count]
    part = pl.program_id(0)

    total = None
    for left, right in zip(lefts, rights):
        left_rows = left[...] if len(left.shape) == 2 else left[0]
        term = matmul(left_rows, right[0])
        total = term if total is None else total + term
    size = pieces[0][3]
    for index in range(4):
        rows = slice(index * row_tile, (index + 1) * row_tile)
        out_ref = keep_ref if index % 2 == 0 else send_ref
        for k in range(total.shape[1] // size):
            first = pl.multiple_of((k * parts + part) * size, size)
            out_ref[index // 2, :, pl.ds(first, size)] = total[
                rows, k * size : (k + 1) * size
            ].astype(out_ref.dtype)


def project(terms):
    rows = terms[0][0].shape[-2] // 4
    parts, _, part_width = terms[0][2].shape
    width = parts * part_width
    pieces = pieces_of(parts, width, lax.axis_size("dp"))
    left_specs, right_specs = [], []
    for acts, kind, weight, first, units in terms:
        if kind is None:
            left_specs.append(whole(acts.shape))
        else:
            left_specs.append(
                pl.BlockSpec(
                    (1, *acts.shape[1:]), lambda j, k=kind: (k, 0, 0), pipeline_mode=pl.Buffered(1)
                )
            )
        right_specs.append(
            pl.BlockSpec((1, units, part_width), lambda j, f=first // units: (j, f, 0))
        )
    out_spec = whole((2, rows, width))
    return pl.pallas_call(
        functools.partial(project_kernel, pieces, rows, parts),
        grid=(parts,),
        out_shape=[
            jax.ShapeDtypeStruct((2, rows, width), jnp.float32),
            jax.ShapeDtypeStruct((2, rows, width), jnp.bfloat16),
        ],
        in_specs=left_specs + right_specs,
        out_specs=[out_spec, out_spec],
        compiler_params=params(),
        cost_estimate=small_cost(),
    )(*[t[0] for t in terms], *[t[2] for t in terms])


def weight_grad_kernel(pieces, cuts, counts, left_ref, *refs):
    out_ref, right_all, sems = refs[sum(counts) :]
    step = pl.program_id(0)

    @pl.when(step == 0)
    def _():
        first = 0
        for k, count in enumerate(counts):
            fetch(refs[first : first + count], right_all.at[k], sems.at[k])
            first += count

    left = left_ref[...].reshape(left_ref.shape[-2:])
    for k, (start, stop) in enumerate(cuts):

        @pl.when(step == start)
        def _():
            first = sum(counts[:k])
            for copy in copies_of(refs[first : first + counts[k]], right_all.at[k], sems.at[k]):
                copy.wait()

        @pl.when((step >= start) & (step < stop))
        def _():
            store_grad(pieces, out_ref, low(mat_rows(left, right_all[k])))


def weight_grad(parts, left, *rights):
    width = rights[0][0][0].shape[1]
    counts = tuple(len(row_parts) for row_parts, _ in rights)
    rows, units = left.shape[-2:]
    tile = unit_tile(units)
    tiles = units // tile
    pieces = pieces_of(parts, width, lax.axis_size("dp"))
    cuts, first = [], 0
    for _, kinds in rights:
        cuts.append((first, first + kinds * tiles))
        first += kinds * tiles
    if left.ndim == 3:
        left_spec = pl.BlockSpec((1, rows, tile), lambda i: (i // tiles, 0, i % tiles))
    else:
        left_spec = pl.BlockSpec((rows, tile), lambda i: (0, i))
    return pl.pallas_call(
        functools.partial(weight_grad_kernel, pieces, tuple(cuts), counts),
        grid=(first,),
        out_shape=jax.ShapeDtypeStruct((parts, first * tile, width // parts), jnp.bfloat16),
        in_specs=[left_spec] + [anywhere()] * sum(counts),
        out_specs=pl.BlockSpec((parts, tile, width // parts), lambda i: (0, i, 0)),
        scratch_shapes=[
            pltpu.VMEM((len(rights), rows, width), jnp.bfloat16),
            pltpu.SemaphoreType.DMA((len(rights), max(counts))),
        ],
        compiler_params=params(),
        cost_estimate=small_cost(),
    )(left, *[part for row_parts, _ in rights for part in row_parts])


def turn(values):
    half = values.shape[-1] // 2
    return jnp.concatenate([values[:, half:], values[:, :half]], axis=-1)


def heads_kernel(
    pieces, q_heads, kv_heads, *refs
):
    normed_parts, (weight_ref, gain_q, gain_k, cos_ref, sin_ref) = refs[:4], refs[4:9]
    raw, rot, value, normed_all, weight_all, sems = refs[9:]
    width = gain_q.shape[1]
    rows = normed_parts[0].shape[0]

    @pl.when(pl.program_id(0) == 0)
    def _():
        fetch(normed_parts, normed_all, sems)
        weight_all[...] = side_by_side(pieces, weight_ref)

    for i, copy in enumerate(copies_of(normed_parts, normed_all, sems)):
        pl.when(pl.program_id(0) == i)(copy.wait)
    here = pl.ds(pl.multiple_of(pl.program_id(0) * rows, rows), rows)
    out = mat_cols(normed_all[here, :], weight_all[...])
    for head in range(q_heads + kv_heads):
        columns = slice(head * width, (head + 1) * width)
        unit = out[:, columns]
        gain = gain_q[...] if head < q_heads else gain_k[...]
        normed = (
            unit * lax.rsqrt(jnp.mean(unit * unit, axis=-1, keepdims=True) + EPSILON) * gain
        )
        raw[:, columns] = unit
        rot[:, columns] = low(normed * cos_ref[...] + turn(normed) * sin_ref[...])
    value[...] = low(out[:, (q_heads + kv_heads) * width :])


def heads(normed_parts, weight, gain_query, gain_key, cos, sin, q_heads, kv_heads):
    part_rows, width = normed_parts[0].shape
    rows = 4 * part_rows
    parts, _, part_width = weight.shape
    head_width = gain_query.shape[1]
    units = (q_heads + 2 * kv_heads) * head_width
    tile = rows // 4
    qk = (q_heads + kv_heads) * head_width
    kv = kv_heads * head_width

    def rows_spec(columns):
        return pl.BlockSpec((tile, columns), lambda i: (i, 0))

    return pl.pallas_call(
        functools.partial(
            heads_kernel, pieces_of(parts, width, lax.axis_size("dp")), q_heads, kv_heads
        ),
        grid=(4,),
        out_shape=[
            jax.ShapeDtypeStruct((rows, qk), jnp.float32),
            jax.ShapeDtypeStruct((rows, qk), jnp.bfloat16),
            jax.ShapeDtypeStruct((rows, kv), jnp.bfloat16),
        ],
        in_specs=[
            *[anywhere()] * 4,
            whole((parts, units, part_width)),
            whole((1, head_width)),
            whole((1, head_width)),
            rows_spec(head_width),
            rows_spec(head_width),
        ],
        out_specs=[rows_spec(qk), rows_spec(qk), rows_spec(kv)],
        scratch_shapes=[
            pltpu.VMEM((rows, width), jnp.bfloat16),
            pltpu.VMEM((units, width), jnp.bfloat16),
            pltpu.SemaphoreType.DMA((4,)),
        ],
        compiler_params=params(),
        cost_estimate=small_cost(),
    )(*normed_parts, weight, gain_query, gain_key, cos, sin)


def mask_of(row_ref, column_ref):
    allowed = (row_ref[0, :, 0:1] == column_ref[0, 0:1, :]) & (
        column_ref[0, 1:2, :] <= row_ref[0, :, 1:2]
    )
    return jnp.where(allowed, 0.0, -1e30)


def probabilities(query, key, mask, live, scale):
    masked = mat_cols(query, key) * scale + mask
    weights = jnp.exp(masked - jnp.max(masked, axis=-1, keepdims=True))
    total = jnp.sum(weights, axis=-1, keepdims=True)
    return weights * (live / total)


def attend_kernel(scale, q_ref, k_ref, v_ref, row_ref, column_ref, out_ref, mask_ref):
    width = k_ref.shape[1]

    @pl.when(pl.program_id(1) == 0)
    def _():
        mask_ref[...] = mask_of(row_ref, column_ref)

    live = 1.0 - wide(row_ref[0, :, 2:3])
    for head in range(q_ref.shape[1] // width):
        columns = slice(head * width, (head + 1) * width)
        probs = probabilities(q_ref[:, columns], k_ref[...], mask_ref[...], live, scale)
        out_ref[:, columns] = low(matmul(low(probs), v_ref[...]))


def attention_specs(rows, head_width, q_heads, kv_heads):
    group_rows = rows // 2
    per = q_heads // kv_heads
    query = pl.BlockSpec((group_rows, per * head_width), lambda g, k: (g, k))
    key = pl.BlockSpec((group_rows, head_width), lambda g, k: (g, q_heads + k))
    value = pl.BlockSpec((group_rows, head_width), lambda g, k: (g, k))
    row_marks = pl.BlockSpec((1, group_rows, 8), lambda g, k: (g, 0, 0))
    column_marks = pl.BlockSpec((1, 8, group_rows), lambda g, k: (g, 0, 0))
    return query, key, value, row_marks, column_marks


def attend(rot, value, row_marks, column_marks, head_width, q_heads, kv_heads):
    rows = rot.shape[0]
    query, key, value_spec, row_spec, column_spec = attention_specs(
        rows, head_width, q_heads, kv_heads
    )
    return pl.pallas_call(
        functools.partial(attend_kernel, head_width ** (-0.5)),
        grid=(2, kv_heads),
        out_shape=jax.ShapeDtypeStruct((rows, q_heads * head_width), jnp.bfloat16),
        in_specs=[query, key, value_spec, row_spec, column_spec],
        out_specs=query,
        scratch_shapes=[pltpu.VMEM((rows // 2, rows // 2), jnp.float32)],
        compiler_params=params(),
        cost_estimate=small_cost(),
    )(rot, rot, value, row_marks, column_marks)


def head_back(grad, raw, gain, cos, sin):
    grad = grad * cos - turn(grad) * sin
    scale = lax.rsqrt(jnp.mean(raw * raw, axis=-1, keepdims=True) + EPSILON)
    unit = raw * scale
    through = grad * gain
    raw_grad = scale * (through - unit * jnp.mean(through * unit, axis=-1, keepdims=True))
    return low(raw_grad), jnp.sum(grad * unit, axis=0, keepdims=True)


def attend_back_kernel(
    pieces,
    scale,
    q_heads,
    kv_heads,
    cot_a,
    cot_b,
    cot_c,
    cot_d,
    weight_ref,
    q_ref,
    k_ref,
    v_ref,
    q_raw,
    k_raw,
    row_ref,
    column_ref,
    gain_q,
    gain_k,
    cos_ref,
    sin_ref,
    grad_ref,
    gain_ref,
    cot_all,
    mask_ref,
    sems,
):
    group, kv = pl.program_id(0), pl.program_id(1)
    cot_parts = (cot_a, cot_b, cot_c, cot_d)
    rows, width = k_ref.shape
    per = q_heads // kv_heads

    @pl.when((group == 0) & (kv == 0))
    def _():
        gain_ref[...] = jnp.zeros_like(gain_ref)
        fetch(cot_parts, cot_all, sems)

    @pl.when(kv == 0)
    def _():
        mask_ref[...] = mask_of(row_ref, column_ref)

    for i, copy in enumerate(copies_of(cot_parts, cot_all, sems)):
        pl.when((group == i // 2) & (kv == 0))(copy.wait)

    live = 1.0 - wide(row_ref[0, :, 2:3])
    here = pl.ds(pl.multiple_of(group * rows, rows), rows)
    context_grad = low(mat_cols(cot_all[here, :], side_by_side(pieces, weight_ref)))
    key, value, cos, sin = k_ref[...], v_ref[...], cos_ref[...], sin_ref[...]
    key_grad = value_grad = None
    gain_sum = None
    for head in range(per):
        columns = slice(head * width, (head + 1) * width)
        query, grad = q_ref[:, columns], context_grad[:, columns]
        probs = probabilities(query, key, mask_ref[...], live, scale)
        prob_grad = mat_cols(grad, value)
        part = mat_rows(low(probs), grad)
        value_grad = part if value_grad is None else value_grad + part
        score_grad = low(
            probs * (prob_grad - jnp.sum(probs * prob_grad, axis=-1, keepdims=True))
        )
        part = mat_rows(score_grad, query)
        key_grad = part if key_grad is None else key_grad + part
        query_grad, gain_part = head_back(
            matmul(score_grad, key) * scale, q_raw[:, columns], gain_q[...], cos, sin
        )
        gain_sum = gain_part if gain_sum is None else gain_sum + gain_part
        first = pl.multiple_of((kv * per + head) * width, width)
        grad_ref[here, pl.ds(first, width)] = query_grad
    key_out, gain_part = head_back(key_grad * scale, k_raw[...], gain_k[...], cos, sin)
    gain_ref[0:1, :] += gain_sum
    gain_ref[1:2, :] += gain_part
    grad_ref[here, pl.ds(pl.multiple_of((q_heads + kv) * width, width), width)] = key_out
    first = pl.multiple_of((q_heads + kv_heads + kv) * width, width)
    grad_ref[here, pl.ds(first, width)] = low(value_grad)


def attend_back(
    cot_parts, weight, rot, value, raw, row_marks, column_marks, gain_query, gain_key, cos, sin,
    q_heads, kv_heads,
):
    part_rows, width = cot_parts[0].shape
    rows = 4 * part_rows
    parts, _, part_width = weight.shape
    head_width = gain_query.shape[1]
    units = q_heads * head_width // kv_heads
    first = (q_heads + 2 * kv_heads) * head_width // units
    group_rows = rows // 2
    query, key, value_spec, row_spec, column_spec = attention_specs(
        rows, head_width, q_heads, kv_heads
    )
    columns = (q_heads + 2 * kv_heads) * head_width

    def group_spec(size):
        return pl.BlockSpec((group_rows, size), lambda g, k: (g, 0))

    return pl.pallas_call(
        functools.partial(
            attend_back_kernel,
            pieces_of(parts, width, lax.axis_size("dp")),
            head_width ** (-0.5),
            q_heads,
            kv_heads,
        ),
        grid=(2, kv_heads),
        out_shape=[
            jax.ShapeDtypeStruct((rows, columns), jnp.bfloat16),
            jax.ShapeDtypeStruct((8, head_width), jnp.float32),
        ],
        in_specs=[
            *[anywhere()] * 4,
            pl.BlockSpec((parts, units, part_width), lambda g, k: (0, first + k, 0)),
            query,
            key,
            value_spec,
            query,
            key,
            row_spec,
            column_spec,
            whole((1, head_width)),
            whole((1, head_width)),
            group_spec(head_width),
            group_spec(head_width),
        ],
        out_specs=[whole((rows, columns)), whole((8, head_width))],
        scratch_shapes=[
            pltpu.VMEM((rows, width), jnp.bfloat16),
            pltpu.VMEM((group_rows, group_rows), jnp.float32),
            pltpu.SemaphoreType.DMA((4,)),
        ],
        compiler_params=params(),
        cost_estimate=large_cost(),
    )(
        *cot_parts, weight, rot, rot, value, raw, raw, row_marks, column_marks,
        gain_query, gain_key, cos, sin,
    )


def norm_back_kernel(mine, mate, values, gain, cot, total_ref, low_ref, gain_ref):
    @pl.when(pl.program_id(0) == 0)
    def _():
        gain_ref[...] = jnp.zeros_like(gain_ref)

    grad = mine[...] + wide(mate[...])
    rows = values[...]
    scale = lax.rsqrt(jnp.mean(rows * rows, axis=-1, keepdims=True) + EPSILON)
    unit = rows * scale
    through = grad * gain[...]
    total = wide(cot[...]) + scale * (
        through - unit * jnp.mean(through * unit, axis=-1, keepdims=True)
    )
    total_ref[...] = total
    low_ref[...] = low(total)
    gain_ref[...] += jnp.sum(grad * unit, axis=0, keepdims=True)


def norm_back(mine, mate, values, gain, cot):
    rows, width = values.shape
    tile = 64
    block = pl.BlockSpec((tile, width), lambda i: (i, 0))
    total, total_low, gain_grad = pl.pallas_call(
        norm_back_kernel,
        grid=(rows // tile,),
        out_shape=[
            jax.ShapeDtypeStruct((rows, width), jnp.float32),
            jax.ShapeDtypeStruct((rows, width), jnp.bfloat16),
            jax.ShapeDtypeStruct((1, width), jnp.float32),
        ],
        in_specs=[block, block, block, whole((1, width)), block],
        out_specs=[block, block, whole((1, width))],
        compiler_params=params(),
        cost_estimate=small_cost(),
    )(mine, mate, values, gain[None, :], cot)
    return total, total_low, gain_grad[0]


class Sequence:
    def __init__(self):
        self.last = ()

    def tie(self, *values):
        out = lax.optimization_barrier((*values, *self.last))[: len(values)]
        return out[0] if len(values) == 1 else out

    def mark(self, *values):
        self.last = values
        return values[0] if len(values) == 1 else values

    def wait(self, *values):
        out = self.tie(*values)
        return self.mark(out) if len(values) == 1 else self.mark(*out)


def swap_core(values):
    return lax.ppermute(values, "tensor", [(0, 1), (1, 0)])


def outer_bits():
    size = lax.axis_size("dp")
    return [1 << i for i in range(size.bit_length() - 1) if (1 << i) > PAIR]


def xy_groups():
    size = lax.axis_size("dp")
    return [[first + i for i in range(4)] for first in range(0, size, 4)]


def far_masks():
    masks = [0, PAIR]
    for bit in outer_bits():
        masks = masks + [m ^ bit for m in masks]
    return masks


def near_start(own, other):
    return [exchange(other if m & PAIR else own, m) for m in far_masks()[1:]]


def near_end(own, received):
    blocks = [own, *received]
    for bit in [PAIR] + outer_bits():
        blocks = [in_turn(x, y, 1, bit) for x, y in zip(blocks[::2], blocks[1::2])]
    return blocks[0]


def outer_start(block):
    return exchange(block, outer_bits()[0])


def outer_end(block, received):
    first, *others = outer_bits()
    block = in_turn(block, received, 1, first)
    for bit in others:
        block = in_turn(block, exchange(block, bit), 1, bit)
    return block


def gather_weight(block):
    return lax.all_gather(block, "dp", axis_index_groups=xy_groups(), axis=0)


def near_x_y(block):
    return (exchange(block, X_BIT), exchange(block, Y_BIT))


def far_x_y(from_x, from_y):
    half = from_x.shape[1] // 2
    return (exchange(from_y[:, :half], X_BIT), exchange(from_x[:, half:], Y_BIT))


def assemble_kernel(slot_ref, own_ref, x_ref, y_ref, left_ref, right_ref, out_ref):
    own, from_x, from_y = own_ref[...], x_ref[...], y_ref[...]
    far = jnp.concatenate([left_ref[...], right_ref[...]], axis=1)
    x_side, y_side = slot_ref[0] % 2 == 1, slot_ref[0] // 2 == 1
    near = [jnp.where(x_side, from_x, own), jnp.where(x_side, own, from_x)]
    other = [jnp.where(x_side, far, from_y), jnp.where(x_side, from_y, far)]
    for k in range(2):
        out_ref[k] = jnp.where(y_side, other[k], near[k])
        out_ref[2 + k] = jnp.where(y_side, near[k], other[k])


def assemble(block, from_x, from_y, left, right):
    units, columns = block.shape
    tile = unit_tile(units)
    slot = (lax.axis_index("dp") & (X_BIT | Y_BIT)).reshape(1).astype(jnp.int32)

    def rows_of(size):
        return pl.BlockSpec((tile, size), lambda i: (i, 0))

    return pl.pallas_call(
        assemble_kernel,
        grid=(units // tile,),
        out_shape=jax.ShapeDtypeStruct((4, units, columns), block.dtype),
        in_specs=[pl.BlockSpec(memory_space=pltpu.SMEM)]
        + [rows_of(columns)] * 3
        + [rows_of(columns // 2)] * 2,
        out_specs=pl.BlockSpec((4, tile, columns), lambda i: (0, i, 0)),
        compiler_params=params(),
        cost_estimate=small_cost(),
    )(slot, block, from_x, from_y, left, right)


def scatter_grad(full):
    total = lax.psum_scatter(
        full, "dp", axis_index_groups=xy_groups(), scatter_dimension=0
    )
    return total.reshape(total.shape[-2:])


def part_of(full, flip):
    place = (lax.axis_index("dp") & (X_BIT | Y_BIT)) ^ flip
    return lax.dynamic_index_in_dim(full, place, 0, keepdims=False)


def scatter_near(full):
    half = full.shape[1] // 2
    far = part_of(full, X_BIT | Y_BIT)
    by_x, by_y = part_of(full, X_BIT), part_of(full, Y_BIT)
    return (
        exchange(jnp.concatenate([far[:half], by_x[:half]], axis=0), X_BIT),
        exchange(jnp.concatenate([far[half:], by_y[half:]], axis=0), Y_BIT),
        by_x[half:],
        by_y[:half],
    )


def scatter_far(from_x, from_y, x_rest, y_rest):
    half = x_rest.shape[0]
    x_bottom = exchange(low(wide(x_rest) + wide(from_y[:half])), X_BIT)
    y_top = exchange(low(wide(y_rest) + wide(from_x[:half])), Y_BIT)
    return (x_bottom, y_top, from_x[half:], from_y[half:])


def scatter_end(full, x_bottom, y_top, x_top, y_bottom):
    own = wide(part_of(full, 0))
    half = own.shape[0] // 2
    return jnp.concatenate(
        [
            own[:half] + wide(x_top) + wide(y_top),
            own[half:] + wide(x_bottom) + wide(y_bottom),
        ],
        axis=0,
    )


def split_side(total, bit):
    size = total.shape[1] // 2
    side = bit_side(bit)
    keep = lax.dynamic_slice_in_dim(total, side * size, size, 1)
    send = lax.dynamic_slice_in_dim(total, (1 - side) * size, size, 1)
    return (wide(keep), low(send))


def outer_scatter_start(total):
    first, *others = outer_bits()
    for bit in reversed(others):
        keep, send = split_side(total, bit)
        total = keep + wide(exchange(send, bit))
    keep, send = split_side(total, first)
    return (keep, exchange(send, first))


def team_scatter_start(keep, received):
    keep, send = split_side(keep + wide(received), PAIR)
    return (keep, exchange(send, PAIR))


def last_start(total):
    masks = far_masks()
    size = total.shape[1] // len(masks)
    place = lax.axis_index("dp") // 4

    def columns(mask):
        return lax.dynamic_slice_in_dim(total, (place ^ (mask // 4)) * size, size, 1)

    return [wide(columns(0))] + [exchange(low(columns(m)), m) for m in masks[1:]]


def last_end(own, received):
    mine, other = own, None
    for mask, values in zip(far_masks()[1:], received):
        if mask & PAIR:
            other = wide(values) if other is None else other + wide(values)
        else:
            mine = mine + wide(values)
    return mine, other


def team_halves(projected):
    keep, send = projected
    received = swap_core(send)
    return (keep[0] + wide(received[0]), low(keep[1] + wide(received[1])))


def near_sum(values):
    values = values + swap_core(values)
    for bit in (X_BIT, Y_BIT):
        values = values + exchange(values, bit)
    return values


def far_sum(values):
    for bit in [PAIR] + outer_bits():
        values = values + exchange(values, bit)
    return values


def per_device(
    tokens,
    seq_ends,
    w_query,
    w_key,
    w_value,
    w_out,
    w_gate,
    w_up,
    w_down,
    gain_attn,
    gain_mlp,
    gain_query,
    gain_key,
    cotangent,
):
    rows_dev, width = tokens.shape
    core = lax.axis_index("tensor")
    side = team_side()
    parts = len(xy_groups()[0])
    head_width = gain_query.shape[0]
    seq = Sequence()

    def halves(weight, axis):
        size = weight.shape[axis] // 2
        return (
            lax.dynamic_slice_in_dim(weight, side * size, size, axis),
            lax.dynamic_slice_in_dim(weight, (1 - side) * size, size, axis),
        )

    q_half, k_half, v_half = halves(w_query, 1), halves(w_key, 1), halves(w_value, 1)
    q_cols, kv_cols = q_half[0].shape[1], k_half[0].shape[1]
    qkv_cols = q_cols + 2 * kv_cols
    q_heads, kv_heads = q_cols // head_width, kv_cols // head_width
    out_half = halves(w_out, 0)
    attn_own, attn_other = [
        jnp.concatenate(
            [jnp.concatenate([q_half[s], k_half[s], v_half[s]], axis=1).T, out_half[s]], axis=0
        )
        for s in (0, 1)
    ]
    ends_mate = exchange(wide(seq_ends), PAIR)
    attn_far = near_start(attn_own, attn_other)
    g_half, u_half, d_half = halves(w_gate, 1), halves(w_up, 1), halves(w_down, 0)
    all_units = g_half[0].shape[1]
    units = all_units // MLP_PARTS

    def mlp_side(s):
        gate, up, down = g_half[s].T, u_half[s].T, d_half[s]
        cuts = [slice(c * units, (c + 1) * units) for c in range(MLP_PARTS)]
        return [
            jnp.concatenate([w[cut] for w in (gate, up, down)], axis=0) for cut in cuts
        ]

    token_float = to_order(wide(tokens))
    cot_float = to_order(wide(cotangent))
    gain_attn_o, gain_mlp_o = to_order(gain_attn), to_order(gain_mlp)
    near = jnp.arange(rows_dev, dtype=jnp.int32)
    slots = jnp.concatenate([core * rows_dev + near, (1 - core) * rows_dev + near])
    layouts = [token_layout(e, slots) for e in (seq_ends[0], ends_mate[0].astype(jnp.int32))]
    segment = jnp.stack([s for s, _ in layouts])
    positions = jnp.concatenate([p for _, p in layouts])
    live_group = segment < seq_ends.shape[1]
    live_mine = wide(live_group)[0, :rows_dev, None]

    normed, attn_norm_pull = jax.vjp(rms_norm, token_float, gain_attn_o)
    normed_low = low(normed)
    normed_mate = exchange(lax.optimization_barrier((normed_low, ends_mate))[0], PAIR)
    normed_core = swap_core(normed_low)
    branch_low = low(live_mine * cot_float)
    cosine_table, sine_table = rope_tables(positions, head_width)
    cos = jnp.concatenate([cosine_table, cosine_table], axis=1)
    sin = jnp.concatenate([-sine_table, sine_table], axis=1)
    slots_both = jnp.stack([slots, slots])
    marks = [
        jnp.where(live_group, segment, -1),
        slots_both,
        1 - live_group.astype(jnp.int32),
    ] + [jnp.zeros_like(segment)] * 5
    row_marks = jnp.stack(marks, axis=2)
    column_marks = jnp.stack([segment, slots_both] + marks[3:] + marks[3:4], axis=1)
    gain_q, gain_k = gain_query[None, :], gain_key[None, :]
    mlp_own, mlp_other = mlp_side(0), mlp_side(1)
    rest_other = jnp.concatenate(mlp_other[1:], axis=0)
    first_pair = exchange(mlp_other[0], PAIR)
    seq.mark(cos, sin, row_marks, column_marks, branch_low, rest_other, *mlp_own)

    first_pair, *attn_far = seq.wait(first_pair, *attn_far)
    attn_near = near_end(attn_own, attn_far)
    attn_x, attn_y = near_x_y(attn_near)
    first_two = in_turn(mlp_own[0], first_pair, 1)
    first_far = outer_start(first_two)
    rest_pair = exchange(seq.tie(rest_other), PAIR)
    attn_x, attn_y, first_far, normed_mate = seq.wait(attn_x, attn_y, first_far, normed_mate)
    attn_left, attn_right = far_x_y(attn_x, attn_y)
    normed_all = (normed_low, normed_core, normed_mate, swap_core(normed_mate))
    attn_left, attn_right, rest_pair = seq.wait(attn_left, attn_right, rest_pair)
    second_two, third_two = [
        in_turn(mlp_own[c], rest_pair[(c - 1) * 3 * units : c * 3 * units], 1)
        for c in range(1, MLP_PARTS)
    ]
    second_far = outer_start(second_two)
    half_rows = rows_dev // 2
    branch_a = exchange(seq.tie(branch_low[:half_rows]), PAIR)
    branch_core = swap_core(branch_low)
    first_near = seq.tie(outer_end(first_two, first_far))
    first_x, first_y = near_x_y(first_near)
    full_attn = assemble(attn_near, attn_x, attn_y, attn_left, attn_right)
    qk_raw, qk_rot, value_low = heads(
        normed_all, full_attn, gain_q, gain_k, cos, sin, q_heads, kv_heads
    )
    value_low = seq.mark(value_low)
    second_far, branch_a, first_x, first_y = seq.wait(second_far, branch_a, first_x, first_y)
    mlp_full = [None, gather_weight(outer_end(second_two, second_far))]
    first_left, first_right = far_x_y(first_x, first_y)
    third_far = outer_start(seq.tie(third_two))
    branch_b = exchange(seq.tie(branch_low[half_rows:]), PAIR)
    context_low = seq.mark(
        attend(
            qk_rot, seq.tie(value_low), row_marks, column_marks, head_width, q_heads, kv_heads
        )
    )
    keep, send = project([(context_low, None, full_attn, qkv_cols, q_cols)])
    seq.mark(send)
    third_far, branch_b, first_left, first_right = seq.wait(
        third_far, branch_b, first_left, first_right
    )
    attn_mine, attn_mate = team_halves((keep, seq.tie(send)))
    mlp_full.append(gather_weight(outer_end(third_two, third_far)))
    seq.mark(attn_mate)
    attn_mate = exchange(attn_mate, PAIR)
    mlp_full[0] = seq.mark(
        assemble(seq.tie(first_near), first_x, first_y, first_left, first_right)
    )
    branch_all = (
        branch_low, branch_core, branch_a, branch_b, swap_core(branch_a), swap_core(branch_b)
    )
    attn_mate = seq.wait(attn_mate)
    hidden_in = token_float + (attn_mine + wide(attn_mate))
    mlp_low = seq.mark(low(rms_norm(hidden_in, gain_mlp_o)))
    mlp_row_mate = exchange(mlp_low, PAIR)
    mlp_row_mate = seq.wait(mlp_row_mate)
    mlp_all = (mlp_low, swap_core(mlp_low), mlp_row_mate, swap_core(mlp_row_mate))
    all_acts, mlp_scattered = [], []
    acts, grad_full = mlp_units(mlp_all, branch_all, mlp_full[0], True)
    all_acts.append(acts)
    grad_full = seq.mark(grad_full)
    mlp_scattered.append(scatter_grad(grad_full))
    mlp_full[1] = seq.wait(mlp_full[1])
    acts, grad_full = mlp_units(mlp_all, branch_all, mlp_full[1], True)
    all_acts.append(acts)
    grad_full = seq.mark(grad_full)
    mlp_scattered.append(scatter_grad(grad_full))
    mlp_full[2] = seq.wait(mlp_full[2])
    (acts,) = mlp_units(mlp_all, branch_all, mlp_full[2], False)
    all_acts.append(acts)
    terms = [
        (a, kind, w, kind * units, units) for a, w in zip(all_acts, mlp_full) for kind in (0, 1)
    ]
    back_mine, back_mate = team_halves(project(terms))
    seq.mark(back_mate)
    back_mate = exchange(back_mate, PAIR)
    terms = [(seq.tie(a), 2, w, 2 * units, units) for a, w in zip(all_acts, mlp_full)]
    sum_keep, sum_send = project(terms)
    seq.mark(sum_send)
    back_mate, mlp_scattered[0] = seq.wait(back_mate, mlp_scattered[0])
    hidden_grad_total, cot_low, gain_mlp_part = norm_back(
        back_mine, back_mate, hidden_in, gain_mlp_o, to_order(cotangent)
    )
    cot_low = seq.mark(cot_low)
    cot_mate = exchange(cot_low, PAIR)
    cot_core = swap_core(cot_low)
    grad_full = seq.mark(weight_grad(parts, seq.tie(acts), (mlp_all, 2), (branch_all, 1)))
    mlp_scattered.append(scatter_grad(grad_full))
    cot_mate, mlp_scattered[1] = seq.wait(cot_mate, mlp_scattered[1])
    early = last_start(jnp.concatenate(mlp_scattered[:2], axis=0))
    cot_all = (cot_low, cot_core, cot_mate, swap_core(cot_mate))
    out_grad = seq.mark(weight_grad(parts, context_low, (cot_all, 1)))
    out_scattered = scatter_grad(out_grad)
    qkv_grad, gain_parts = attend_back(
        cot_all, seq.tie(full_attn), qk_rot, value_low, qk_raw, row_marks, column_marks,
        gain_q, gain_k, cos, sin, q_heads, kv_heads,
    )
    qkv_full = seq.mark(weight_grad(parts, qkv_grad, (normed_all, 1)))
    qkv_steps = scatter_near(qkv_full)
    keep, send = project([(seq.tie(qkv_grad), None, full_attn, 0, qkv_cols)])
    seq.mark(send)
    mlp_scattered[2], *early = seq.wait(mlp_scattered[2], *early)
    late_keep, late_far = outer_scatter_start(mlp_scattered[2])
    token_mine, token_mate = team_halves((keep, seq.tie(send)))
    token_mate = seq.mark(token_mate)
    token_mate = exchange(token_mate, PAIR)
    qkv_steps = seq.wait(*qkv_steps)
    qkv_steps = scatter_far(*qkv_steps)
    sum_mine, sum_mate = team_halves((sum_keep, seq.tie(sum_send)))
    token_mate, late_far = seq.wait(token_mate, late_far)
    late_mine, late_other = team_scatter_start(late_keep, late_far)
    sum_mate = exchange(seq.tie(sum_mate), PAIR)
    early_mine, early_other = last_end(early[0], early[1:])
    attn_back = token_mine + wide(token_mate)
    token_from, gain_attn_part = attn_norm_pull(attn_back)
    grad_tokens = from_order(hidden_grad_total + token_from)
    gain_parts = near_sum(
        jnp.concatenate(
            [
                from_order(gain_attn_part),
                from_order(gain_mlp_part),
                gain_parts[0],
                gain_parts[1],
            ]
        )
    )
    seq.mark(grad_tokens, gain_parts)
    out_scattered, *qkv_steps = seq.wait(out_scattered, *qkv_steps)
    final = last_start(
        jnp.concatenate([scatter_end(qkv_full, *qkv_steps), wide(out_scattered)], axis=0)
    )
    late_other, sum_mate = seq.wait(late_other, sum_mate)
    late_other = wide(late_other)
    mlp_sum = sum_mine + wide(sum_mate)
    out_tokens = from_order(low(hidden_in + live_mine * mlp_sum))
    gain_sums = far_sum(seq.tie(gain_parts))
    cut = 3 * units
    teams = [
        (early_mine[:cut], early_other[:cut]),
        (early_mine[cut:], early_other[cut:]),
        (late_mine, late_other),
    ]

    def pick(pair, start, stop):
        return in_turn(pair[0][start:stop], pair[1][start:stop], 0)

    def units_of(kind):
        cut = slice(kind * units, (kind + 1) * units)
        return in_turn(
            jnp.concatenate([keep[cut] for keep, _ in teams], axis=0),
            jnp.concatenate([other[cut] for _, other in teams], axis=0),
            0,
        )

    grad_gate = units_of(0).T
    grad_up = units_of(1).T
    grad_down = units_of(2)
    seq.mark(grad_gate, grad_up, grad_down, out_tokens, grad_tokens)
    final = seq.wait(*final)
    attn_team = last_end(final[0], final[1:])
    grad_out = pick(attn_team, qkv_cols, qkv_cols + q_cols)
    grad_query = pick(attn_team, 0, q_cols).T
    grad_key = pick(attn_team, q_cols, q_cols + kv_cols).T
    grad_value = pick(attn_team, q_cols + kv_cols, qkv_cols).T
    return (
        out_tokens,
        grad_tokens,
        grad_query,
        grad_key,
        grad_value,
        grad_out,
        grad_gate,
        grad_up,
        grad_down,
        gain_sums[:width],
        gain_sums[width : 2 * width],
        gain_sums[2 * width : 2 * width + head_width],
        gain_sums[2 * width + head_width :],
    )


def solution(mesh):
    weight_in = P("dp", "tensor")
    weight_out = P("tensor", "dp")
    rows = P(("dp", "tensor"), None)
    weights = (weight_in, weight_in, weight_in, weight_out, weight_in, weight_in, weight_out)
    gains = (P(), P(), P(), P())
    return jax.shard_map(
        per_device,
        mesh=mesh,
        in_specs=(rows, P("dp", None), *weights, *gains, rows),
        out_specs=(rows, rows, *weights, *gains),
        check_vma=False,
    )
```

```python
import functools

import jax
import jax.numpy as jnp
from jax import lax
from jax.experimental import pallas as pl
from jax.experimental.pallas import tpu as pltpu
from jax.sharding import PartitionSpec as P

EPSILON = 1e-06
ROPE_BASE = 1000000.0
X_BIT, Y_BIT, PAIR = 1, 2, 4
MLP_PARTS = 3
LANES = 128


def rms_norm(values, gain_vec):
    return (
        values * lax.rsqrt(jnp.mean(values * values, axis=-1, keepdims=True) + EPSILON) * gain_vec
    )


def rope_tables(positions, width):
    half_width = width // 2
    frequency = ROPE_BASE ** (-2.0 * jnp.arange(half_width, dtype=jnp.float32) / width)
    angles = positions.astype(jnp.float32)[:, None] * frequency[None, :]
    return (jnp.cos(angles), jnp.sin(angles))


def token_layout(seq_ends, token_index):
    segment = jnp.sum((token_index[:, None] >= seq_ends[None, :]).astype(jnp.int32), axis=1)
    starts = jnp.concatenate([jnp.zeros((1,), jnp.int32), seq_ends[:-1]])
    onehot = (segment[:, None] == jnp.arange(seq_ends.shape[0], dtype=jnp.int32)[None, :]).astype(
        jnp.int32
    )
    positions = token_index - jnp.sum(onehot * starts[None, :], axis=1)
    return (segment, positions)


def matmul(left, right):
    return jnp.dot(left, right, preferred_element_type=jnp.float32)


def mat_rows(left, right):
    return lax.dot_general(
        left, right, (((0,), (0,)), ((), ())), preferred_element_type=jnp.float32
    )


def mat_cols(left, right):
    return lax.dot_general(
        left, right, (((1,), (1,)), ((), ())), preferred_element_type=jnp.float32
    )


def low(values):
    return values.astype(jnp.bfloat16)


def wide(values):
    return values.astype(jnp.float32)


def exchange(values, mask):
    size = lax.axis_size("dp")
    return lax.ppermute(values, "dp", [(i, i ^ mask) for i in range(size)])


def bit_side(bit):
    return jnp.minimum(lax.axis_index("dp") & bit, 1)


def team_side():
    return bit_side(PAIR)


def in_turn(mine, theirs, axis, bit=PAIR):
    return jnp.where(
        bit_side(bit) == 0,
        jnp.concatenate([mine, theirs], axis=axis),
        jnp.concatenate([theirs, mine], axis=axis),
    )


VMEM_BYTES = 56 * 1024 * 1024
UNIT_TILE = 256


def params():
    return pltpu.CompilerParams(vmem_limit_bytes=VMEM_BYTES)


def small_cost():
    return pl.CostEstimate(flops=1000, bytes_accessed=1000, transcendentals=0)


def large_cost():
    return pl.CostEstimate(flops=400_000_000_000, bytes_accessed=1000, transcendentals=0)


def unit_tile(units):
    return UNIT_TILE if units % UNIT_TILE == 0 else units


def whole(shape):
    return pl.BlockSpec(shape, lambda *_: (0,) * len(shape), pipeline_mode=pl.Buffered(1))


def anywhere():
    return pl.BlockSpec(memory_space=pl.ANY)


def in_lanes(width):
    return (width // lax.axis_size("dp")) % LANES == 0


def to_order(values, parts=4):
    width = values.shape[-1]
    if in_lanes(width):
        return values
    devices = lax.axis_size("dp")
    split = values.reshape(*values.shape[:-1], devices // parts, parts, width // devices)
    return jnp.swapaxes(split, -2, -3).reshape(values.shape)


def from_order(values, parts=4):
    width = values.shape[-1]
    if in_lanes(width):
        return values
    devices = lax.axis_size("dp")
    split = values.reshape(*values.shape[:-1], parts, devices // parts, width // devices)
    return jnp.swapaxes(split, -2, -3).reshape(values.shape)


def pieces_of(parts, width, devices):
    part_width, block = width // parts, width // devices
    if block % LANES:
        return [(p, 0, p * part_width, part_width) for p in range(parts)]
    return [
        (d % parts, (d // parts) * block, d * block, block) for d in range(devices)
    ]


def side_by_side(pieces, ref):
    return jnp.concatenate([ref[p][:, at : at + size] for p, at, _, size in pieces], axis=1)


def copies_of(parts, scratch, sems):
    copies, first = [], 0
    for i, part in enumerate(parts):
        rows = part.shape[0]
        copies.append(
            pltpu.make_async_copy(part, scratch.at[pl.ds(first, rows), :], sems.at[i])
        )
        first += rows
    return copies


def fetch(parts, scratch, sems):
    copies = copies_of(parts, scratch, sems)
    for copy in copies:
        copy.start()
    return copies


def pieces_in(parts, start, stop):
    found, first = [], 0
    for i, part in enumerate(parts):
        if start <= first < stop:
            found.append(i)
        first += part.shape[0]
    return found


def rows_in(parts):
    return sum(part.shape[0] for part in parts)


def hidden_rows(rows, mlp_all, branch_all, gate_w, up_w, down_w, store):
    mlp_rows = mlp_all[rows, :]
    gate_proj = mat_cols(mlp_rows, gate_w)
    up_proj = mat_cols(mlp_rows, up_w)
    hidden_grad = mat_cols(branch_all[rows, :], down_w)
    sigmoid_gate = 1.0 / (1.0 + jnp.exp(-gate_proj))
    silu_gate = gate_proj * sigmoid_gate
    store(
        0,
        rows,
        low(hidden_grad * up_proj * sigmoid_gate * (1.0 + gate_proj * (1.0 - sigmoid_gate))),
    )
    store(1, rows, low(hidden_grad * silu_gate))
    store(2, rows, low(silu_gate * up_proj))


def store_grad(pieces, out_ref, grad):
    for p, at, first, size in pieces:
        out_ref[p, :, at : at + size] = grad[:, first : first + size]


def mlp_kernel(pieces, tiles, with_grad, counts, *refs):
    count = sum(counts)
    mlp_parts, branch_parts = refs[: counts[0]], refs[counts[0] : count]
    weights = refs[count : count + 3]
    if with_grad:
        acts_ref, grad_ref, mlp_all, branch_all, acts_all, sems = refs[count + 3 :]
    else:
        acts_ref, mlp_all, branch_all, sems = refs[count + 3 :]
    step = pl.program_id(0)
    total = mlp_all.shape[0]
    rows = total // 4

    def store(kind, where, values):
        acts_ref[kind, where, :] = values
        if with_grad:
            acts_all[step, kind, where, :] = values

    def sides():
        return [side_by_side(pieces, w) for w in weights]

    @pl.when(step == 0)
    def _():
        mlp_copies = fetch(mlp_parts, mlp_all, sems.at[0])
        branch_copies = fetch(branch_parts, branch_all, sems.at[1])
        sides_now = sides()
        for first in range(0, total, rows):
            for i in pieces_in(mlp_parts, first, first + rows):
                mlp_copies[i].wait()
            for i in pieces_in(branch_parts, first, first + rows):
                branch_copies[i].wait()
            hidden_rows(slice(first, first + rows), mlp_all, branch_all, *sides_now, store)

    @pl.when((step > 0) & (step < tiles))
    def _():
        hidden_rows(slice(0, total), mlp_all, branch_all, *sides(), store)

    if not with_grad:
        return

    @pl.when((step >= tiles) & (step < 3 * tiles))
    def _():
        index = step - tiles
        acts = acts_all[lax.rem(index, tiles), lax.div(index, tiles)]
        store_grad(pieces, grad_ref, low(mat_rows(acts, mlp_all[...])))

    @pl.when(step >= 3 * tiles)
    def _():
        acts = acts_all[step - 3 * tiles, 2]
        store_grad(pieces, grad_ref, low(mat_rows(acts, branch_all[...])))


def mlp_units(mlp_parts, branch_parts, weight, with_grad):
    rows, width = rows_in(mlp_parts), mlp_parts[0].shape[1]
    counts = (len(mlp_parts), len(branch_parts))
    parts, units3, part_width = weight.shape
    units = units3 // 3
    tile = unit_tile(units)
    tiles = units // tile
    pieces = pieces_of(parts, width, lax.axis_size("dp"))

    def weight_spec(kind):
        return pl.BlockSpec(
            (parts, tile, part_width), lambda i: (0, kind * tiles + jnp.minimum(i, tiles - 1), 0)
        )

    out_shape = [jax.ShapeDtypeStruct((3, rows, units), jnp.bfloat16)]
    out_specs = [pl.BlockSpec((3, rows, tile), lambda i: (0, 0, jnp.minimum(i, tiles - 1)))]
    scratch = [pltpu.VMEM((rows, width), jnp.bfloat16)] * 2
    if with_grad:
        out_shape.append(jax.ShapeDtypeStruct(weight.shape, jnp.bfloat16))
        out_specs.append(
            pl.BlockSpec((parts, tile, part_width), lambda i: (0, jnp.maximum(i - tiles, 0), 0))
        )
        scratch.append(pltpu.VMEM((tiles, 3, rows, tile), jnp.bfloat16))
    return pl.pallas_call(
        functools.partial(mlp_kernel, pieces, tiles, with_grad, counts),
        grid=(4 * tiles if with_grad else tiles,),
        out_shape=out_shape,
        in_specs=[anywhere()] * sum(counts) + [weight_spec(k) for k in range(3)],
        out_specs=out_specs,
        scratch_shapes=scratch + [pltpu.SemaphoreType.DMA((2, max(counts)))],
        compiler_params=params(),
        cost_estimate=small_cost(),
    )(*mlp_parts, *branch_parts, weight, weight, weight)


def project_kernel(pieces, row_tile, parts, *refs):
    keep_ref, send_ref = refs[-2:]
    count = (len(refs) - 2) // 2
    lefts, rights = refs[:count], refs[count : 2 * count]
    part = pl.program_id(0)

    total = None
    for left, right in zip(lefts, rights):
        left_rows = left[...] if len(left.shape) == 2 else left[0]
        term = matmul(left_rows, right[0])
        total = term if total is None else total + term
    size = pieces[0][3]
    for index in range(4):
        rows = slice(index * row_tile, (index + 1) * row_tile)
        out_ref = keep_ref if index % 2 == 0 else send_ref
        for k in range(total.shape[1] // size):
            first = pl.multiple_of((k * parts + part) * size, size)
            out_ref[index // 2, :, pl.ds(first, size)] = total[
                rows, k * size : (k + 1) * size
            ].astype(out_ref.dtype)


def project(terms):
    rows = terms[0][0].shape[-2] // 4
    parts, _, part_width = terms[0][2].shape
    width = parts * part_width
    pieces = pieces_of(parts, width, lax.axis_size("dp"))
    left_specs, right_specs = [], []
    for acts, kind, weight, first, units in terms:
        if kind is None:
            left_specs.append(whole(acts.shape))
        else:
            left_specs.append(
                pl.BlockSpec(
                    (1, *acts.shape[1:]), lambda j, k=kind: (k, 0, 0), pipeline_mode=pl.Buffered(1)
                )
            )
        right_specs.append(
            pl.BlockSpec((1, units, part_width), lambda j, f=first // units: (j, f, 0))
        )
    out_spec = whole((2, rows, width))
    return pl.pallas_call(
        functools.partial(project_kernel, pieces, rows, parts),
        grid=(parts,),
        out_shape=[
            jax.ShapeDtypeStruct((2, rows, width), jnp.float32),
            jax.ShapeDtypeStruct((2, rows, width), jnp.bfloat16),
        ],
        in_specs=left_specs + right_specs,
        out_specs=[out_spec, out_spec],
        compiler_params=params(),
        cost_estimate=small_cost(),
    )(*[t[0] for t in terms], *[t[2] for t in terms])


def weight_grad_kernel(pieces, cuts, counts, left_ref, *refs):
    out_ref, right_all, sems = refs[sum(counts) :]
    step = pl.program_id(0)

    @pl.when(step == 0)
    def _():
        first = 0
        for k, count in enumerate(counts):
            fetch(refs[first : first + count], right_all.at[k], sems.at[k])
            first += count

    left = left_ref[...].reshape(left_ref.shape[-2:])
    for k, (start, stop) in enumerate(cuts):

        @pl.when(step == start)
        def _():
            first = sum(counts[:k])
            for copy in copies_of(refs[first : first + counts[k]], right_all.at[k], sems.at[k]):
                copy.wait()

        @pl.when((step >= start) & (step < stop))
        def _():
            store_grad(pieces, out_ref, low(mat_rows(left, right_all[k])))


def weight_grad(parts, left, *rights):
    width = rights[0][0][0].shape[1]
    counts = tuple(len(row_parts) for row_parts, _ in rights)
    rows, units = left.shape[-2:]
    tile = unit_tile(units)
    tiles = units // tile
    pieces = pieces_of(parts, width, lax.axis_size("dp"))
    cuts, first = [], 0
    for _, kinds in rights:
        cuts.append((first, first + kinds * tiles))
        first += kinds * tiles
    if left.ndim == 3:
        left_spec = pl.BlockSpec((1, rows, tile), lambda i: (i // tiles, 0, i % tiles))
    else:
        left_spec = pl.BlockSpec((rows, tile), lambda i: (0, i))
    return pl.pallas_call(
        functools.partial(weight_grad_kernel, pieces, tuple(cuts), counts),
        grid=(first,),
        out_shape=jax.ShapeDtypeStruct((parts, first * tile, width // parts), jnp.bfloat16),
        in_specs=[left_spec] + [anywhere()] * sum(counts),
        out_specs=pl.BlockSpec((parts, tile, width // parts), lambda i: (0, i, 0)),
        scratch_shapes=[
            pltpu.VMEM((len(rights), rows, width), jnp.bfloat16),
            pltpu.SemaphoreType.DMA((len(rights), max(counts))),
        ],
        compiler_params=params(),
        cost_estimate=small_cost(),
    )(left, *[part for row_parts, _ in rights for part in row_parts])


def turn(values):
    half = values.shape[-1] // 2
    return jnp.concatenate([values[:, half:], values[:, :half]], axis=-1)


def heads_kernel(
    pieces, q_heads, kv_heads, *refs
):
    normed_parts, (weight_ref, gain_q, gain_k, cos_ref, sin_ref) = refs[:4], refs[4:9]
    raw, rot, value, normed_all, weight_all, sems = refs[9:]
    width = gain_q.shape[1]
    rows = normed_parts[0].shape[0]

    @pl.when(pl.program_id(0) == 0)
    def _():
        fetch(normed_parts, normed_all, sems)
        weight_all[...] = side_by_side(pieces, weight_ref)

    for i, copy in enumerate(copies_of(normed_parts, normed_all, sems)):
        pl.when(pl.program_id(0) == i)(copy.wait)
    here = pl.ds(pl.multiple_of(pl.program_id(0) * rows, rows), rows)
    out = mat_cols(normed_all[here, :], weight_all[...])
    for head in range(q_heads + kv_heads):
        columns = slice(head * width, (head + 1) * width)
        unit = out[:, columns]
        gain = gain_q[...] if head < q_heads else gain_k[...]
        normed = (
            unit * lax.rsqrt(jnp.mean(unit * unit, axis=-1, keepdims=True) + EPSILON) * gain
        )
        raw[:, columns] = unit
        rot[:, columns] = low(normed * cos_ref[...] + turn(normed) * sin_ref[...])
    value[...] = low(out[:, (q_heads + kv_heads) * width :])


def heads(normed_parts, weight, gain_query, gain_key, cos, sin, q_heads, kv_heads):
    part_rows, width = normed_parts[0].shape
    rows = 4 * part_rows
    parts, _, part_width = weight.shape
    head_width = gain_query.shape[1]
    units = (q_heads + 2 * kv_heads) * head_width
    tile = rows // 4
    qk = (q_heads + kv_heads) * head_width
    kv = kv_heads * head_width

    def rows_spec(columns):
        return pl.BlockSpec((tile, columns), lambda i: (i, 0))

    return pl.pallas_call(
        functools.partial(
            heads_kernel, pieces_of(parts, width, lax.axis_size("dp")), q_heads, kv_heads
        ),
        grid=(4,),
        out_shape=[
            jax.ShapeDtypeStruct((rows, qk), jnp.float32),
            jax.ShapeDtypeStruct((rows, qk), jnp.bfloat16),
            jax.ShapeDtypeStruct((rows, kv), jnp.bfloat16),
        ],
        in_specs=[
            *[anywhere()] * 4,
            whole((parts, units, part_width)),
            whole((1, head_width)),
            whole((1, head_width)),
            rows_spec(head_width),
            rows_spec(head_width),
        ],
        out_specs=[rows_spec(qk), rows_spec(qk), rows_spec(kv)],
        scratch_shapes=[
            pltpu.VMEM((rows, width), jnp.bfloat16),
            pltpu.VMEM((units, width), jnp.bfloat16),
            pltpu.SemaphoreType.DMA((4,)),
        ],
        compiler_params=params(),
        cost_estimate=small_cost(),
    )(*normed_parts, weight, gain_query, gain_key, cos, sin)


def mask_of(row_ref, column_ref):
    allowed = (row_ref[0, :, 0:1] == column_ref[0, 0:1, :]) & (
        column_ref[0, 1:2, :] <= row_ref[0, :, 1:2]
    )
    return jnp.where(allowed, 0.0, -1e30)


def probabilities(query, key, mask, live, scale):
    masked = mat_cols(query, key) * scale + mask
    weights = jnp.exp(masked - jnp.max(masked, axis=-1, keepdims=True))
    total = jnp.sum(weights, axis=-1, keepdims=True)
    return weights * (live / total)


def attend_kernel(scale, q_ref, k_ref, v_ref, row_ref, column_ref, out_ref, mask_ref):
    width = k_ref.shape[1]

    @pl.when(pl.program_id(1) == 0)
    def _():
        mask_ref[...] = mask_of(row_ref, column_ref)

    live = 1.0 - wide(row_ref[0, :, 2:3])
    for head in range(q_ref.shape[1] // width):
        columns = slice(head * width, (head + 1) * width)
        probs = probabilities(q_ref[:, columns], k_ref[...], mask_ref[...], live, scale)
        out_ref[:, columns] = low(matmul(low(probs), v_ref[...]))


def attention_specs(rows, head_width, q_heads, kv_heads):
    group_rows = rows // 2
    per = q_heads // kv_heads
    query = pl.BlockSpec((group_rows, per * head_width), lambda g, k: (g, k))
    key = pl.BlockSpec((group_rows, head_width), lambda g, k: (g, q_heads + k))
    value = pl.BlockSpec((group_rows, head_width), lambda g, k: (g, k))
    row_marks = pl.BlockSpec((1, group_rows, 8), lambda g, k: (g, 0, 0))
    column_marks = pl.BlockSpec((1, 8, group_rows), lambda g, k: (g, 0, 0))
    return query, key, value, row_marks, column_marks


def attend(rot, value, row_marks, column_marks, head_width, q_heads, kv_heads):
    rows = rot.shape[0]
    query, key, value_spec, row_spec, column_spec = attention_specs(
        rows, head_width, q_heads, kv_heads
    )
    return pl.pallas_call(
        functools.partial(attend_kernel, head_width ** (-0.5)),
        grid=(2, kv_heads),
        out_shape=jax.ShapeDtypeStruct((rows, q_heads * head_width), jnp.bfloat16),
        in_specs=[query, key, value_spec, row_spec, column_spec],
        out_specs=query,
        scratch_shapes=[pltpu.VMEM((rows // 2, rows // 2), jnp.float32)],
        compiler_params=params(),
        cost_estimate=small_cost(),
    )(rot, rot, value, row_marks, column_marks)


def head_back(grad, raw, gain, cos, sin):
    grad = grad * cos - turn(grad) * sin
    scale = lax.rsqrt(jnp.mean(raw * raw, axis=-1, keepdims=True) + EPSILON)
    unit = raw * scale
    through = grad * gain
    raw_grad = scale * (through - unit * jnp.mean(through * unit, axis=-1, keepdims=True))
    return low(raw_grad), jnp.sum(grad * unit, axis=0, keepdims=True)


def attend_back_kernel(
    pieces,
    scale,
    q_heads,
    kv_heads,
    cot_a,
    cot_b,
    cot_c,
    cot_d,
    weight_ref,
    q_ref,
    k_ref,
    v_ref,
    q_raw,
    k_raw,
    row_ref,
    column_ref,
    gain_q,
    gain_k,
    cos_ref,
    sin_ref,
    grad_ref,
    gain_ref,
    cot_all,
    mask_ref,
    sems,
):
    group, kv = pl.program_id(0), pl.program_id(1)
    cot_parts = (cot_a, cot_b, cot_c, cot_d)
    rows, width = k_ref.shape
    per = q_heads // kv_heads

    @pl.when((group == 0) & (kv == 0))
    def _():
        gain_ref[...] = jnp.zeros_like(gain_ref)
        fetch(cot_parts, cot_all, sems)

    @pl.when(kv == 0)
    def _():
        mask_ref[...] = mask_of(row_ref, column_ref)

    for i, copy in enumerate(copies_of(cot_parts, cot_all, sems)):
        pl.when((group == i // 2) & (kv == 0))(copy.wait)

    live = 1.0 - wide(row_ref[0, :, 2:3])
    here = pl.ds(pl.multiple_of(group * rows, rows), rows)
    context_grad = low(mat_cols(cot_all[here, :], side_by_side(pieces, weight_ref)))
    key, value, cos, sin = k_ref[...], v_ref[...], cos_ref[...], sin_ref[...]
    key_grad = value_grad = None
    gain_sum = None
    for head in range(per):
        columns = slice(head * width, (head + 1) * width)
        query, grad = q_ref[:, columns], context_grad[:, columns]
        probs = probabilities(query, key, mask_ref[...], live, scale)
        prob_grad = mat_cols(grad, value)
        part = mat_rows(low(probs), grad)
        value_grad = part if value_grad is None else value_grad + part
        score_grad = low(
            probs * (prob_grad - jnp.sum(probs * prob_grad, axis=-1, keepdims=True))
        )
        part = mat_rows(score_grad, query)
        key_grad = part if key_grad is None else key_grad + part
        query_grad, gain_part = head_back(
            matmul(score_grad, key) * scale, q_raw[:, columns], gain_q[...], cos, sin
        )
        gain_sum = gain_part if gain_sum is None else gain_sum + gain_part
        first = pl.multiple_of((kv * per + head) * width, width)
        grad_ref[here, pl.ds(first, width)] = query_grad
    key_out, gain_part = head_back(key_grad * scale, k_raw[...], gain_k[...], cos, sin)
    gain_ref[0:1, :] += gain_sum
    gain_ref[1:2, :] += gain_part
    grad_ref[here, pl.ds(pl.multiple_of((q_heads + kv) * width, width), width)] = key_out
    first = pl.multiple_of((q_heads + kv_heads + kv) * width, width)
    grad_ref[here, pl.ds(first, width)] = low(value_grad)


def attend_back(
    cot_parts, weight, rot, value, raw, row_marks, column_marks, gain_query, gain_key, cos, sin,
    q_heads, kv_heads,
):
    part_rows, width = cot_parts[0].shape
    rows = 4 * part_rows
    parts, _, part_width = weight.shape
    head_width = gain_query.shape[1]
    units = q_heads * head_width // kv_heads
    first = (q_heads + 2 * kv_heads) * head_width // units
    group_rows = rows // 2
    query, key, value_spec, row_spec, column_spec = attention_specs(
        rows, head_width, q_heads, kv_heads
    )
    columns = (q_heads + 2 * kv_heads) * head_width

    def group_spec(size):
        return pl.BlockSpec((group_rows, size), lambda g, k: (g, 0))

    return pl.pallas_call(
        functools.partial(
            attend_back_kernel,
            pieces_of(parts, width, lax.axis_size("dp")),
            head_width ** (-0.5),
            q_heads,
            kv_heads,
        ),
        grid=(2, kv_heads),
        out_shape=[
            jax.ShapeDtypeStruct((rows, columns), jnp.bfloat16),
            jax.ShapeDtypeStruct((8, head_width), jnp.float32),
        ],
        in_specs=[
            *[anywhere()] * 4,
            pl.BlockSpec((parts, units, part_width), lambda g, k: (0, first + k, 0)),
            query,
            key,
            value_spec,
            query,
            key,
            row_spec,
            column_spec,
            whole((1, head_width)),
            whole((1, head_width)),
            group_spec(head_width),
            group_spec(head_width),
        ],
        out_specs=[whole((rows, columns)), whole((8, head_width))],
        scratch_shapes=[
            pltpu.VMEM((rows, width), jnp.bfloat16),
            pltpu.VMEM((group_rows, group_rows), jnp.float32),
            pltpu.SemaphoreType.DMA((4,)),
        ],
        compiler_params=params(),
        cost_estimate=large_cost(),
    )(
        *cot_parts, weight, rot, rot, value, raw, raw, row_marks, column_marks,
        gain_query, gain_key, cos, sin,
    )


def norm_back_kernel(mine, mate, values, gain, cot, total_ref, low_ref, gain_ref):
    @pl.when(pl.program_id(0) == 0)
    def _():
        gain_ref[...] = jnp.zeros_like(gain_ref)

    grad = mine[...] + wide(mate[...])
    rows = values[...]
    scale = lax.rsqrt(jnp.mean(rows * rows, axis=-1, keepdims=True) + EPSILON)
    unit = rows * scale
    through = grad * gain[...]
    total = wide(cot[...]) + scale * (
        through - unit * jnp.mean(through * unit, axis=-1, keepdims=True)
    )
    total_ref[...] = total
    low_ref[...] = low(total)
    gain_ref[...] += jnp.sum(grad * unit, axis=0, keepdims=True)


def norm_back(mine, mate, values, gain, cot):
    rows, width = values.shape
    tile = 64
    block = pl.BlockSpec((tile, width), lambda i: (i, 0))
    total, total_low, gain_grad = pl.pallas_call(
        norm_back_kernel,
        grid=(rows // tile,),
        out_shape=[
            jax.ShapeDtypeStruct((rows, width), jnp.float32),
            jax.ShapeDtypeStruct((rows, width), jnp.bfloat16),
            jax.ShapeDtypeStruct((1, width), jnp.float32),
        ],
        in_specs=[block, block, block, whole((1, width)), block],
        out_specs=[block, block, whole((1, width))],
        compiler_params=params(),
        cost_estimate=small_cost(),
    )(mine, mate, values, gain[None, :], cot)
    return total, total_low, gain_grad[0]


def split_kernel(side_ref, query, key, value, out, own_ref, other_ref):
    for ref, side in ((own_ref, side_ref[0]), (other_ref, 1 - side_ref[0])):
        first = 0
        for weight in (query, key, value):
            size = weight.shape[1] // 2
            half = weight[:, pl.ds(pl.multiple_of(side * size, size), size)]
            ref[first : first + size, :] = low(wide(half).T)
            first += size
        size = out.shape[0] // 2
        ref[first : first + size, :] = out[pl.ds(pl.multiple_of(side * size, size), size), :]


def split_attention(side, query, key, value, out):
    units = (query.shape[1] + key.shape[1] + value.shape[1] + out.shape[0]) // 2
    shape = jax.ShapeDtypeStruct((units, out.shape[1]), out.dtype)
    return pl.pallas_call(
        split_kernel,
        out_shape=[shape, shape],
        in_specs=[pl.BlockSpec(memory_space=pltpu.SMEM)]
        + [pl.BlockSpec(memory_space=pltpu.VMEM)] * 4,
        out_specs=[pl.BlockSpec(memory_space=pltpu.VMEM)] * 2,
        compiler_params=params(),
        cost_estimate=small_cost(),
    )(side, query, key, value, out)


def finish_kernel(counts, places, side_ref, *refs):
    groups, first = [], 0
    for mine, other in counts:
        groups.append((refs[first : first + mine], refs[first + mine : first + mine + other]))
        first += mine + other
    outs = refs[first:]
    side = side_ref[0]
    for group, row, size, out, place, extent, turned in places:
        for which, parts in zip((side, 1 - side), groups[group]):
            total = None
            for part in parts:
                values = wide(part[row : row + size, :])
                total = values if total is None else total + values
            at = pl.ds(pl.multiple_of(which * extent + place, size), size)
            if turned:
                outs[out][:, at] = total.T
            else:
                outs[out][at, :] = total


def finish(side, groups, places, shapes):
    counts = tuple((len(mine), len(other)) for mine, other in groups)
    parts = [part for mine, other in groups for part in (*mine, *other)]
    return pl.pallas_call(
        functools.partial(finish_kernel, counts, tuple(places)),
        out_shape=[jax.ShapeDtypeStruct(shape, jnp.float32) for shape in shapes],
        in_specs=[pl.BlockSpec(memory_space=pltpu.SMEM)]
        + [pl.BlockSpec(memory_space=pltpu.VMEM)] * len(parts),
        out_specs=[pl.BlockSpec(memory_space=pltpu.VMEM)] * len(shapes),
        compiler_params=params(),
        cost_estimate=small_cost(),
    )(side, *parts)


class Sequence:
    def __init__(self):
        self.last = ()

    def tie(self, *values):
        out = lax.optimization_barrier((*values, *self.last))[: len(values)]
        return out[0] if len(values) == 1 else out

    def mark(self, *values):
        self.last = values
        return values[0] if len(values) == 1 else values

    def wait(self, *values):
        out = self.tie(*values)
        return self.mark(out) if len(values) == 1 else self.mark(*out)


def swap_core(values):
    return lax.ppermute(values, "tensor", [(0, 1), (1, 0)])


def outer_bits():
    size = lax.axis_size("dp")
    return [1 << i for i in range(size.bit_length() - 1) if (1 << i) > PAIR]


def xy_groups():
    size = lax.axis_size("dp")
    return [[first + i for i in range(4)] for first in range(0, size, 4)]


def far_masks():
    masks = [0, PAIR]
    for bit in outer_bits():
        masks = masks + [m ^ bit for m in masks]
    return masks


def near_start(own, other):
    return [exchange(other if m & PAIR else own, m) for m in far_masks()[1:]]


def near_end(own, received):
    blocks = [own, *received]
    for bit in [PAIR] + outer_bits():
        blocks = [in_turn(x, y, 1, bit) for x, y in zip(blocks[::2], blocks[1::2])]
    return blocks[0]


def outer_start(block):
    return exchange(block, outer_bits()[0])


def outer_end(block, received):
    first, *others = outer_bits()
    block = in_turn(block, received, 1, first)
    for bit in others:
        block = in_turn(block, exchange(block, bit), 1, bit)
    return block


def gather_weight(block):
    return lax.all_gather(block, "dp", axis_index_groups=xy_groups(), axis=0)


def near_x_y(block):
    return (exchange(block, X_BIT), exchange(block, Y_BIT))


def far_x_y(from_x, from_y):
    half = from_x.shape[1] // 2
    return (exchange(from_y[:, :half], X_BIT), exchange(from_x[:, half:], Y_BIT))


def assemble_kernel(slot_ref, own_ref, x_ref, y_ref, left_ref, right_ref, out_ref):
    own, from_x, from_y = own_ref[...], x_ref[...], y_ref[...]
    far = jnp.concatenate([left_ref[...], right_ref[...]], axis=1)
    x_side, y_side = slot_ref[0] % 2 == 1, slot_ref[0] // 2 == 1
    near = [jnp.where(x_side, from_x, own), jnp.where(x_side, own, from_x)]
    other = [jnp.where(x_side, far, from_y), jnp.where(x_side, from_y, far)]
    for k in range(2):
        out_ref[k] = jnp.where(y_side, other[k], near[k])
        out_ref[2 + k] = jnp.where(y_side, near[k], other[k])


def assemble(block, from_x, from_y, left, right):
    units, columns = block.shape
    tile = unit_tile(units)
    slot = (lax.axis_index("dp") & (X_BIT | Y_BIT)).reshape(1).astype(jnp.int32)

    def rows_of(size):
        return pl.BlockSpec((tile, size), lambda i: (i, 0))

    return pl.pallas_call(
        assemble_kernel,
        grid=(units // tile,),
        out_shape=jax.ShapeDtypeStruct((4, units, columns), block.dtype),
        in_specs=[pl.BlockSpec(memory_space=pltpu.SMEM)]
        + [rows_of(columns)] * 3
        + [rows_of(columns // 2)] * 2,
        out_specs=pl.BlockSpec((4, tile, columns), lambda i: (0, i, 0)),
        compiler_params=params(),
        cost_estimate=small_cost(),
    )(slot, block, from_x, from_y, left, right)


def scatter_grad(full):
    total = lax.psum_scatter(
        full, "dp", axis_index_groups=xy_groups(), scatter_dimension=0
    )
    return total.reshape(total.shape[-2:])


def part_of(full, flip):
    place = (lax.axis_index("dp") & (X_BIT | Y_BIT)) ^ flip
    return lax.dynamic_index_in_dim(full, place, 0, keepdims=False)


def scatter_near(full):
    half = full.shape[1] // 2
    far = part_of(full, X_BIT | Y_BIT)
    by_x, by_y = part_of(full, X_BIT), part_of(full, Y_BIT)
    return (
        exchange(jnp.concatenate([far[:half], by_x[:half]], axis=0), X_BIT),
        exchange(jnp.concatenate([far[half:], by_y[half:]], axis=0), Y_BIT),
        by_x[half:],
        by_y[:half],
    )


def scatter_far(from_x, from_y, x_rest, y_rest):
    half = x_rest.shape[0]
    x_bottom = exchange(low(wide(x_rest) + wide(from_y[:half])), X_BIT)
    y_top = exchange(low(wide(y_rest) + wide(from_x[:half])), Y_BIT)
    return (x_bottom, y_top, from_x[half:], from_y[half:])


def scatter_end(full, x_bottom, y_top, x_top, y_bottom):
    own = wide(part_of(full, 0))
    half = own.shape[0] // 2
    return jnp.concatenate(
        [
            own[:half] + wide(x_top) + wide(y_top),
            own[half:] + wide(x_bottom) + wide(y_bottom),
        ],
        axis=0,
    )


def split_side(total, bit):
    size = total.shape[1] // 2
    side = bit_side(bit)
    keep = lax.dynamic_slice_in_dim(total, side * size, size, 1)
    send = lax.dynamic_slice_in_dim(total, (1 - side) * size, size, 1)
    return (wide(keep), low(send))


def outer_scatter_start(total):
    first, *others = outer_bits()
    for bit in reversed(others):
        keep, send = split_side(total, bit)
        total = keep + wide(exchange(send, bit))
    keep, send = split_side(total, first)
    return (keep, exchange(send, first))


def team_scatter_start(keep, received):
    keep, send = split_side(keep + wide(received), PAIR)
    return (keep, exchange(send, PAIR))


def last_start(total):
    masks = far_masks()
    size = total.shape[1] // len(masks)
    place = lax.axis_index("dp") // 4

    def columns(mask):
        return lax.dynamic_slice_in_dim(total, (place ^ (mask // 4)) * size, size, 1)

    return [low(columns(0))] + [exchange(low(columns(m)), m) for m in masks[1:]]


def last_parts(own, received):
    masks = far_masks()[1:]
    return (
        [own] + [v for m, v in zip(masks, received) if not m & PAIR],
        [v for m, v in zip(masks, received) if m & PAIR],
    )


def team_halves(projected):
    keep, send = projected
    received = swap_core(send)
    return (keep[0] + wide(received[0]), low(keep[1] + wide(received[1])))


def near_sum(values):
    values = values + swap_core(values)
    for bit in (X_BIT, Y_BIT):
        values = values + exchange(values, bit)
    return values


def far_sum(values):
    for bit in [PAIR] + outer_bits():
        values = values + exchange(values, bit)
    return values


def per_device(
    tokens,
    seq_ends,
    w_query,
    w_key,
    w_value,
    w_out,
    w_gate,
    w_up,
    w_down,
    gain_attn,
    gain_mlp,
    gain_query,
    gain_key,
    cotangent,
):
    rows_dev, width = tokens.shape
    core = lax.axis_index("tensor")
    side = team_side()
    parts = len(xy_groups()[0])
    head_width = gain_query.shape[0]
    seq = Sequence()

    def halves(weight, axis):
        size = weight.shape[axis] // 2
        return (
            lax.dynamic_slice_in_dim(weight, side * size, size, axis),
            lax.dynamic_slice_in_dim(weight, (1 - side) * size, size, axis),
        )

    q_cols, kv_cols = w_query.shape[1] // 2, w_key.shape[1] // 2
    qkv_cols = q_cols + 2 * kv_cols
    q_heads, kv_heads = q_cols // head_width, kv_cols // head_width
    side_arg = side.reshape(1).astype(jnp.int32)
    attn_own, attn_other = split_attention(side_arg, w_query, w_key, w_value, w_out)
    ends_mate = exchange(wide(seq_ends), PAIR)
    attn_far = near_start(attn_own, attn_other)
    g_half, u_half, d_half = halves(w_gate, 1), halves(w_up, 1), halves(w_down, 0)
    all_units = g_half[0].shape[1]
    units = all_units // MLP_PARTS

    def mlp_side(s):
        gate, up, down = g_half[s].T, u_half[s].T, d_half[s]
        cuts = [slice(c * units, (c + 1) * units) for c in range(MLP_PARTS)]
        return [
            jnp.concatenate([w[cut] for w in (gate, up, down)], axis=0) for cut in cuts
        ]

    token_float = to_order(wide(tokens))
    cot_float = to_order(wide(cotangent))
    gain_attn_o, gain_mlp_o = to_order(gain_attn), to_order(gain_mlp)
    near = jnp.arange(rows_dev, dtype=jnp.int32)
    slots = jnp.concatenate([core * rows_dev + near, (1 - core) * rows_dev + near])
    layouts = [token_layout(e, slots) for e in (seq_ends[0], ends_mate[0].astype(jnp.int32))]
    segment = jnp.stack([s for s, _ in layouts])
    positions = jnp.concatenate([p for _, p in layouts])
    live_group = segment < seq_ends.shape[1]
    live_mine = wide(live_group)[0, :rows_dev, None]

    normed, attn_norm_pull = jax.vjp(rms_norm, token_float, gain_attn_o)
    normed_low = low(normed)
    normed_mate = exchange(lax.optimization_barrier((normed_low, ends_mate))[0], PAIR)
    normed_core = swap_core(normed_low)
    branch_low = low(live_mine * cot_float)
    cosine_table, sine_table = rope_tables(positions, head_width)
    cos = jnp.concatenate([cosine_table, cosine_table], axis=1)
    sin = jnp.concatenate([-sine_table, sine_table], axis=1)
    slots_both = jnp.stack([slots, slots])
    marks = [
        jnp.where(live_group, segment, -1),
        slots_both,
        1 - live_group.astype(jnp.int32),
    ] + [jnp.zeros_like(segment)] * 5
    row_marks = jnp.stack(marks, axis=2)
    column_marks = jnp.stack([segment, slots_both] + marks[3:] + marks[3:4], axis=1)
    gain_q, gain_k = gain_query[None, :], gain_key[None, :]
    mlp_own, mlp_other = mlp_side(0), mlp_side(1)
    rest_other = jnp.concatenate(mlp_other[1:], axis=0)
    first_pair = exchange(mlp_other[0], PAIR)
    seq.mark(cos, sin, row_marks, column_marks, branch_low, rest_other, *mlp_own)

    first_pair, *attn_far = seq.wait(first_pair, *attn_far)
    attn_near = near_end(attn_own, attn_far)
    attn_x, attn_y = near_x_y(attn_near)
    first_two = in_turn(mlp_own[0], first_pair, 1)
    first_far = outer_start(first_two)
    rest_pair = exchange(seq.tie(rest_other), PAIR)
    attn_x, attn_y, first_far, normed_mate = seq.wait(attn_x, attn_y, first_far, normed_mate)
    attn_left, attn_right = far_x_y(attn_x, attn_y)
    normed_all = (normed_low, normed_core, normed_mate, swap_core(normed_mate))
    attn_left, attn_right, rest_pair = seq.wait(attn_left, attn_right, rest_pair)
    second_two, third_two = [
        in_turn(mlp_own[c], rest_pair[(c - 1) * 3 * units : c * 3 * units], 1)
        for c in range(1, MLP_PARTS)
    ]
    second_far = outer_start(second_two)
    half_rows = rows_dev // 2
    branch_a = exchange(seq.tie(branch_low[:half_rows]), PAIR)
    branch_core = swap_core(branch_low)
    first_near = seq.tie(outer_end(first_two, first_far))
    first_x, first_y = near_x_y(first_near)
    full_attn = assemble(attn_near, attn_x, attn_y, attn_left, attn_right)
    qk_raw, qk_rot, value_low = heads(
        normed_all, full_attn, gain_q, gain_k, cos, sin, q_heads, kv_heads
    )
    value_low = seq.mark(value_low)
    second_far, branch_a, first_x, first_y = seq.wait(second_far, branch_a, first_x, first_y)
    mlp_full = [None, gather_weight(outer_end(second_two, second_far))]
    first_left, first_right = far_x_y(first_x, first_y)
    third_far = outer_start(seq.tie(third_two))
    branch_b = exchange(seq.tie(branch_low[half_rows:]), PAIR)
    context_low = seq.mark(
        attend(
            qk_rot, seq.tie(value_low), row_marks, column_marks, head_width, q_heads, kv_heads
        )
    )
    keep, send = project([(context_low, None, full_attn, qkv_cols, q_cols)])
    seq.mark(send)
    third_far, branch_b, first_left, first_right = seq.wait(
        third_far, branch_b, first_left, first_right
    )
    attn_mine, attn_mate = team_halves((keep, seq.tie(send)))
    mlp_full.append(gather_weight(outer_end(third_two, third_far)))
    seq.mark(attn_mate)
    attn_mate = exchange(attn_mate, PAIR)
    mlp_full[0] = seq.mark(
        assemble(seq.tie(first_near), first_x, first_y, first_left, first_right)
    )
    branch_all = (
        branch_low, branch_core, branch_a, branch_b, swap_core(branch_a), swap_core(branch_b)
    )
    attn_mate = seq.wait(attn_mate)
    hidden_in = token_float + (attn_mine + wide(attn_mate))
    mlp_low = seq.mark(low(rms_norm(hidden_in, gain_mlp_o)))
    mlp_row_mate = exchange(mlp_low, PAIR)
    mlp_row_mate = seq.wait(mlp_row_mate)
    mlp_all = (mlp_low, swap_core(mlp_low), mlp_row_mate, swap_core(mlp_row_mate))
    all_acts, mlp_scattered = [], []
    acts, grad_full = mlp_units(mlp_all, branch_all, mlp_full[0], True)
    all_acts.append(acts)
    grad_full = seq.mark(grad_full)
    mlp_scattered.append(scatter_grad(grad_full))
    mlp_full[1] = seq.wait(mlp_full[1])
    acts, grad_full = mlp_units(mlp_all, branch_all, mlp_full[1], True)
    all_acts.append(acts)
    grad_full = seq.mark(grad_full)
    mlp_scattered.append(scatter_grad(grad_full))
    mlp_full[2] = seq.wait(mlp_full[2])
    (acts,) = mlp_units(mlp_all, branch_all, mlp_full[2], False)
    all_acts.append(acts)
    terms = [
        (a, kind, w, kind * units, units) for a, w in zip(all_acts, mlp_full) for kind in (0, 1)
    ]
    back_mine, back_mate = team_halves(project(terms))
    seq.mark(back_mate)
    back_mate = exchange(back_mate, PAIR)
    terms = [(seq.tie(a), 2, w, 2 * units, units) for a, w in zip(all_acts, mlp_full)]
    sum_keep, sum_send = project(terms)
    seq.mark(sum_send)
    back_mate, mlp_scattered[0] = seq.wait(back_mate, mlp_scattered[0])
    hidden_grad_total, cot_low, gain_mlp_part = norm_back(
        back_mine, back_mate, hidden_in, gain_mlp_o, to_order(cotangent)
    )
    cot_low = seq.mark(cot_low)
    cot_mate = exchange(cot_low, PAIR)
    cot_core = swap_core(cot_low)
    grad_full = seq.mark(weight_grad(parts, seq.tie(acts), (mlp_all, 2), (branch_all, 1)))
    mlp_scattered.append(scatter_grad(grad_full))
    cot_mate, mlp_scattered[1] = seq.wait(cot_mate, mlp_scattered[1])
    early = last_start(jnp.concatenate(mlp_scattered[:2], axis=0))
    cot_all = (cot_low, cot_core, cot_mate, swap_core(cot_mate))
    out_grad = seq.mark(weight_grad(parts, context_low, (cot_all, 1)))
    out_scattered = scatter_grad(out_grad)
    qkv_grad, gain_parts = attend_back(
        cot_all, seq.tie(full_attn), qk_rot, value_low, qk_raw, row_marks, column_marks,
        gain_q, gain_k, cos, sin, q_heads, kv_heads,
    )
    qkv_full = seq.mark(weight_grad(parts, qkv_grad, (normed_all, 1)))
    qkv_steps = scatter_near(qkv_full)
    keep, send = project([(seq.tie(qkv_grad), None, full_attn, 0, qkv_cols)])
    seq.mark(send)
    mlp_scattered[2], *early = seq.wait(mlp_scattered[2], *early)
    late_keep, late_far = outer_scatter_start(mlp_scattered[2])
    token_mine, token_mate = team_halves((keep, seq.tie(send)))
    token_mate = seq.mark(token_mate)
    token_mate = exchange(token_mate, PAIR)
    qkv_steps = seq.wait(*qkv_steps)
    qkv_steps = scatter_far(*qkv_steps)
    sum_mine, sum_mate = team_halves((sum_keep, seq.tie(sum_send)))
    token_mate, late_far = seq.wait(token_mate, late_far)
    late_mine, late_other = team_scatter_start(late_keep, late_far)
    sum_mate = exchange(seq.tie(sum_mate), PAIR)
    attn_back = token_mine + wide(token_mate)
    token_from, gain_attn_part = attn_norm_pull(attn_back)
    grad_tokens = from_order(hidden_grad_total + token_from)
    gain_parts = near_sum(
        jnp.concatenate(
            [
                from_order(gain_attn_part),
                from_order(gain_mlp_part),
                gain_parts[0],
                gain_parts[1],
            ]
        )
    )
    seq.mark(grad_tokens, gain_parts)
    out_scattered, *qkv_steps = seq.wait(out_scattered, *qkv_steps)
    final = last_start(
        jnp.concatenate([scatter_end(qkv_full, *qkv_steps), wide(out_scattered)], axis=0)
    )
    late_other, sum_mate, *final = seq.wait(late_other, sum_mate, *final)
    mlp_sum = sum_mine + wide(sum_mate)
    out_tokens = from_order(low(hidden_in + live_mine * mlp_sum))
    gain_sums = far_sum(seq.tie(gain_parts))
    where = [(0, 0), (0, 3 * units), (1, 0)]
    grad_gate, grad_up, grad_down = finish(
        side_arg,
        [last_parts(early[0], early[1:]), ([late_mine], [late_other])],
        [
            (group, first + kind * units, units, kind, chunk * units, all_units, kind < 2)
            for chunk, (group, first) in enumerate(where)
            for kind in range(3)
        ],
        [w_gate.shape, w_up.shape, w_down.shape],
    )
    grad_query, grad_key, grad_value, grad_out = finish(
        side_arg,
        [last_parts(final[0], final[1:])],
        [
            (0, 0, q_cols, 0, 0, q_cols, True),
            (0, q_cols, kv_cols, 1, 0, kv_cols, True),
            (0, q_cols + kv_cols, kv_cols, 2, 0, kv_cols, True),
            (0, qkv_cols, q_cols, 3, 0, q_cols, False),
        ],
        [w_query.shape, w_key.shape, w_value.shape, w_out.shape],
    )
    return (
        out_tokens,
        grad_tokens,
        grad_query,
        grad_key,
        grad_value,
        grad_out,
        grad_gate,
        grad_up,
        grad_down,
        gain_sums[:width],
        gain_sums[width : 2 * width],
        gain_sums[2 * width : 2 * width + head_width],
        gain_sums[2 * width + head_width :],
    )


def solution(mesh):
    weight_in = P("dp", "tensor")
    weight_out = P("tensor", "dp")
    rows = P(("dp", "tensor"), None)
    weights = (weight_in, weight_in, weight_in, weight_out, weight_in, weight_in, weight_out)
    gains = (P(), P(), P(), P())
    return jax.shard_map(
        per_device,
        mesh=mesh,
        in_specs=(rows, P("dp", None), *weights, *gains, rows),
        out_specs=(rows, rows, *weights, *gains),
        check_vma=False,
    )
```
